256 devices in a mesh: mem: 64 (over z, y, core), job: 4 (over x).
Axes of the slice: x: 4, y: 4, z: 8, core: 2. Of those that a mesh axis runs over, the one named last changes fastest.
Arguments:
- pair_cost: bfloat16 [12288, 128, 128], P(('mem', 'job')), may hold values from -6 to 6
- pair_coef: bfloat16 [12288, 128, 128], P(('mem', 'job')), may hold values from 0.049804688 to 0.5
- slot_member: int32 [256, 48], P(('mem', 'job')), may hold values from 0 to 31, never falling along the last dimension, each value on 1 to 4 neighbouring positions
- slot_owner: int32 [256, 48, 1], P(('mem', 'job')), may hold values from 0 to 63; in each aligned block of 48 rows (0 to 47, 48 to 95, ..., all dimensions but the last counted through in order) at most 2 rows name the same one
- slot_local: int32 [256, 48], P(('mem', 'job')), may hold values from 0 to 15
- duals: float32 [4096, 128], P(('mem', 'job')), may hold values from 0.1 to 3
- capacity: int32 [4096, 128], P(('mem', 'job')), may hold values from 0 to 39
Outputs:
- primal: bfloat16 [12288, 128, 128], P(('mem', 'job'))
- gradient: float32 [4096, 128], P(('mem', 'job'))
- member_share: float32 [2048, 128], P('mem')
The draws below stay inside these ranges and needn't reach their ends.
Inputs may be any that keep to these rules, and one draw needn't show every extreme that they name: `slot_member`: in each device's row the values never fall, every value appears, none more than 4 times, and one exactly 4 times. `slot_owner`: among the 48 entries of one device no value appears more than 2 times, and in some devices one appears exactly 2 times.
All inputs are finite; a program needn't handle non-finite values.
Results may differ from the reference program's by a relative error of at most 0.001.
Values sent between devices are 32-bit elements; how exact they have to be, the bound alone decides.
No kernel may reach another device: no remote copies, remote signals or barrier semaphores. Data moves between devices by JAX's collectives and lax.ppermute only.
A program may use at most 64 MiB of HBM per device.

```python
import math
import jax
import jax.numpy as jnp
import numpy as np
from jax import lax

BLOCK = 128
CAP = 48
MB_DEV = 32
JB_DEV = 16
SEG_MOST = 4
PEER_MOST = 2
NBLK = 12288
MBLK = 2048
JBLK = 4096
N_MEM = 64
N_JOB = 4


def plant(array, key, least, high):
    place = [jax.random.randint(jax.random.fold_in(key, axis), (), 0, length) for axis, length in enumerate(array.shape)]
    longest = array.shape.index(max(array.shape))
    neighbour = place[:longest] + [(place[longest] + 1) % array.shape[longest]] + place[longest + 1:]
    return array.at[tuple(place)].set(least).at[tuple(neighbour)].set(high)


def shard_levels(key, shape, pieces, least, high):
    def one(position, blocks):
        draws = jax.random.uniform(jax.random.fold_in(jax.random.fold_in(key, 6), position), (blocks,), jnp.float32, least / len(pieces), high / len(pieces))
        return jnp.repeat(jnp.exp(draws), shape[position] // blocks).reshape((-1,) + (1,) * (len(shape) - position - 1))

    factor_of = one(*pieces[0])
    for cut in pieces[1:]:
        factor_of = factor_of * one(*cut)
    return factor_of


def split_up(number_of, total, reach, lean):
    portions = [(1 << 20) // math.isqrt(grade ** lean) + 1 for grade in range(2, number_of + 1)]
    rest, counts = total - reach - (number_of - 1), [1] * (number_of - 1)
    while rest > 0:
        candidates = [i for i in range(number_of - 1) if counts[i] < reach]
        mass, left = sum([portions[i] for i in candidates]), rest
        for i in candidates:
            more = min(reach - counts[i], max(1, left * portions[i] // mass), rest)
            counts[i] = counts[i] + more
            rest = rest - more
    return np.array([reach] + counts)


def uneven(rng, amount, total, limit, slope):
    if amount == 2:
        one = jax.random.randint(rng, (), max(1, total - limit), min(limit, total - 1) + 1)
        return jnp.stack([one, total - one])
    sizes = jnp.asarray(split_up(amount, total, limit, slope), jnp.int32)
    couples = (amount - 1) // 2
    source_of, receiver = sizes[1:1 + 2 * couples:2], sizes[2:2 + 2 * couples:2]
    slack = jnp.minimum(source_of - 1, limit - receiver)
    passed = jax.random.randint(jax.random.fold_in(rng, 1), (couples,), 0, 1 << 20) % (slack + 1)
    sizes = sizes.at[1:1 + 2 * couples:2].set(source_of - passed).at[2:2 + 2 * couples:2].set(receiver + passed)
    return sizes[jax.random.permutation(jax.random.fold_in(rng, 2), amount)]


def shared_out(own_key, own, number, rows, amount, top, limit, skew):
    ranking = jax.random.permutation(own_key, amount)
    crowded, ordinary = shares(amount, rows * top, limit, skew, True), shares(amount, rows * top, limit, skew, False)
    places = jnp.arange(amount)

    def named(sizes, offset_by):
        used = int((sizes > 0).sum())
        fixed = max(1, used // 4)
        moved = fixed + (places - fixed + offset_by * (used - fixed)) % max(1, amount - fixed)
        return jnp.zeros((amount,), jnp.int32).at[ranking[jnp.where(places < fixed, places, moved)]].set(jnp.asarray(sizes, jnp.int32))

    sizes = jnp.where(number % 4 == 0, named(crowded, number // 4), named(ordinary, number - number // 4 - 1))
    mixed = jax.random.permutation(jax.random.fold_in(own, 3), amount)
    giver, receiver = mixed[0:amount // 2 * 2:2], mixed[1:amount // 2 * 2:2]
    room = jnp.minimum(sizes[giver] - 1, limit - sizes[receiver]) // 2
    room = jnp.where((giver == ranking[0]) | (receiver == ranking[0]) | (sizes[receiver] == 0), 0, jnp.maximum(room, 0))
    moved = jax.random.randint(jax.random.fold_in(own, 4), (amount // 2,), 0, 1 << 20) % (room + 1)
    sizes = sizes.at[giver].add(-moved).at[receiver].add(moved)
    items = jnp.searchsorted(jnp.cumsum(sizes), jnp.arange(rows * top), side="right").astype(jnp.int32)
    grid = items.reshape(top, rows).T
    grid = grid[jax.random.permutation(jax.random.fold_in(own, 1), rows)]
    offset_by = jax.random.randint(jax.random.fold_in(own, 2), (rows, 1), 0, top)
    return jnp.take_along_axis(grid, (jnp.arange(top)[None, :] + offset_by) % top, axis=1)


def shares(number_of, total, reach, skew, full):
    weights = [(1 << 20) // math.isqrt(standing ** skew) + 1 for standing in range(1, number_of + 1)]
    largest = reach if full else min(reach, max(-(-total // number_of), total * weights[0] // sum(weights)))
    least = 1 if total - largest >= number_of - 1 else 0
    holding, rest = [largest] + [least] * (number_of - 1), total - largest - least * (number_of - 1)
    while rest > 0:
        candidates = [i for i in range(1, number_of) if holding[i] < largest] or [i for i in range(1, number_of) if holding[i] < reach]
        mass, budget = sum([weights[i] for i in candidates]), rest
        for i in candidates:
            addition = min(reach - holding[i], max(1, budget * weights[i] // mass), rest)
            holding[i] = holding[i] + addition
            rest = rest - addition
    return np.array(holding)


def gaussian(key, extent, width, bound, shards=(), kind=jnp.bfloat16):
    level = shard_levels(key, extent, shards, -0.22, 0.18) if shards else 1.0
    array = jax.random.normal(key, extent, jnp.float32) * width * level
    return jnp.minimum(jnp.maximum(array, -bound), bound).astype(kind)


def setup_inputs(seed: int = 0) -> dict:
    keys = jax.random.split(jax.random.key(seed), 8)
    pair_cost = gaussian(keys[0], (NBLK, BLOCK, BLOCK), 1.0, 6.0, ((0, 256),))
    pair_coef = jnp.clip(jnp.exp(math.log(0.5) - 2.306499 * jax.random.uniform(keys[1], (NBLK, BLOCK, BLOCK), jnp.float32) ** shard_levels(keys[1], (NBLK, BLOCK, BLOCK), ((0, 256),), -0.2, 0.2)), 0.049804688, 0.5).astype(jnp.bfloat16)
    slot_member = jax.vmap(lambda own: jnp.searchsorted(jnp.cumsum(uneven(own, MB_DEV, CAP, SEG_MOST, 2)), jnp.arange(CAP), side="right"))(jax.random.split(keys[2], (N_MEM * N_JOB))).reshape((N_MEM * N_JOB, CAP)).astype(jnp.int32)
    slot_owner_keys = jax.random.split(jax.random.fold_in(keys[3], 1), (N_MEM * N_JOB) * CAP // CAP)
    slot_owner_turns = jax.random.permutation(jax.random.fold_in(keys[3], 3), (N_MEM * N_JOB) * CAP // CAP)
    slot_owner = jax.vmap(lambda own, number: shared_out(jax.random.fold_in(keys[3], 2), own, number, CAP, N_MEM, 1, PEER_MOST, 2))(slot_owner_keys, slot_owner_turns).reshape((N_MEM * N_JOB, CAP, 1))
    slot_local = plant(jax.random.randint(keys[4], (N_MEM * N_JOB, CAP), 0, JB_DEV), jax.random.fold_in(keys[4], 1), 0, JB_DEV - 1).astype(jnp.int32)
    duals = jnp.clip(jnp.exp(math.log(3.0) - 3.4011974 * jax.random.uniform(keys[5], (JBLK, BLOCK), jnp.float32) ** shard_levels(keys[5], (JBLK, BLOCK), ((0, 256),), -0.2, 0.2)), 0.1, 3.0)
    capacity = plant(jax.random.randint(keys[6], (JBLK, BLOCK), 0, 40), jax.random.fold_in(keys[6], 1), 0, 39).astype(jnp.int32)
    return dict(pair_cost=pair_cost, pair_coef=pair_coef, slot_member=slot_member, slot_owner=slot_owner, slot_local=slot_local, duals=duals, capacity=capacity)


RIDGE = 1.0


def slot_terms(packed):
    pair_cost, pair_coef, dual_rows = packed
    reduced = pair_cost.astype(jnp.float32) + pair_coef.astype(jnp.float32) * dual_rows[:, None, :]
    allocation = jnp.clip(-reduced / RIDGE, 0.0, 1.0)
    column_part = jnp.sum(pair_coef.astype(jnp.float32) * allocation, axis=1)
    row_part = jnp.sum(allocation, axis=2)
    return allocation.astype(jnp.bfloat16), column_part, row_part


def reference(pair_cost, pair_coef, slot_member, slot_owner, slot_local, duals, capacity):
    device = jnp.arange(N_MEM * N_JOB, dtype=jnp.int32)
    column = device % N_JOB
    job_block = (slot_owner[:, :, 0] * N_JOB + column[:, None]) * JB_DEV + slot_local
    member_block = (device // N_JOB)[:, None] * MB_DEV + slot_member
    dual_rows = duals[job_block.reshape(-1)].reshape(N_MEM * N_JOB, CAP, BLOCK)
    cost_dev = pair_cost.reshape(N_MEM * N_JOB, CAP, BLOCK, BLOCK)
    coef_dev = pair_coef.reshape(N_MEM * N_JOB, CAP, BLOCK, BLOCK)
    primal, column_part, row_part = lax.map(slot_terms, (cost_dev, coef_dev, dual_rows))
    totals = jax.ops.segment_sum(column_part.reshape(-1, BLOCK), job_block.reshape(-1).astype(jnp.int32), num_segments=JBLK)
    gradient = totals - capacity.astype(jnp.float32)
    members = jax.ops.segment_sum(row_part.reshape(-1, BLOCK), member_block.reshape(-1).astype(jnp.int32), num_segments=MBLK)
    member_share = members / BLOCK
    return primal.reshape(NBLK, BLOCK, BLOCK), gradient, member_share
```

```python
import jax
import jax.numpy as jnp
from jax import lax
from jax.experimental import pallas as pl
from jax.experimental.pallas import tpu as pltpu
from jax.sharding import Mesh, PartitionSpec as P

Z, Y, C, X = 8, 4, 2, 4
CAP = 48
BLOCK = 128
MB_DEV = 32
JB_DEV = 16
MEM = Z * Y * C
ROWS = 4
RIDGE = 1.0


def allocate_kernel(
    owner_ref, local_ref, member_ref, rows_ref, cost_ref, coef_ref,
    primal_ref, send_ref, member_out_ref, count_ref,
):
    send_ref[...] = jnp.full((MEM * ROWS, BLOCK), -1.0, jnp.float32)
    member_out_ref[...] = jnp.zeros((MB_DEV, BLOCK), jnp.float32)
    ones = jnp.ones((8, BLOCK), jnp.bfloat16)

    def clear(i, carry):
        count_ref[i] = 0
        return carry

    lax.fori_loop(0, MEM, clear, 0, unroll=8)

    def block(s, carry):
        owner = owner_ref[0, s]
        local = local_ref[0, s]
        member = member_ref[0, s]
        row = (owner & 1) * (Z * Y * JB_DEV) + (owner >> 1) * JB_DEV + local
        minus_dual = -rows_ref[pl.ds(row, 1), :]
        cost = cost_ref[s].astype(jnp.float32)
        coef = coef_ref[s].astype(jnp.float32)
        alloc = jnp.minimum(jnp.maximum(coef * minus_dual - cost, 0.0), 1.0)
        high = alloc.astype(jnp.bfloat16)
        primal_ref[s] = high
        rest = (alloc - high.astype(jnp.float32)).astype(jnp.bfloat16)
        column = jnp.sum(coef * alloc, axis=0, keepdims=True)
        k = count_ref[owner]
        count_ref[owner] = k + 1
        place = owner * ROWS + k
        send_ref[pl.ds(place, 1), :] = column
        send_ref[pl.ds(place + 2, 1), :] = jnp.full((1, BLOCK), local.astype(jnp.float32))
        dims = (((1,), (1,)), ((), ()))
        sums = lax.dot_general(ones, high, dims, preferred_element_type=jnp.float32)
        sums = sums + lax.dot_general(ones, rest, dims, preferred_element_type=jnp.float32)
        member_out_ref[pl.ds(member, 1), :] += sums[0:1]
        return carry

    lax.fori_loop(0, CAP, block, 0, unroll=2)


def finish_kernel(recv_ref, m0_ref, m1_ref, m2_ref, m3_ref, capacity_ref, gradient_ref, share_ref):
    share_ref[...] = ((m0_ref[...] + m1_ref[...]) + (m2_ref[...] + m3_ref[...])) * (1.0 / BLOCK)
    sub = lax.broadcasted_iota(jnp.int32, (8, BLOCK), 0) % 4
    data = sub < 2
    totals = [jnp.zeros((8, BLOCK), jnp.float32) for _ in range(JB_DEV)]
    for i in range(MEM * ROWS // 8):
        got = recv_ref[i * 8:(i + 1) * 8, :]
        name = jnp.where(data, pltpu.roll(got, 6, 0), -1.0)
        for k in range(JB_DEV):
            totals[k] = totals[k] + jnp.where(name == float(k), got, 0.0)
    summed = jnp.concatenate([jnp.sum(t, axis=0, keepdims=True) for t in totals], axis=0)
    gradient_ref[...] = summed - capacity_ref[...].astype(jnp.float32)


def per_device(pair_cost, pair_coef, slot_member, slot_owner, slot_local, duals, capacity):
    vmem = pl.BlockSpec(memory_space=pltpu.VMEM)
    smem = pl.BlockSpec(memory_space=pltpu.SMEM)
    copies = jnp.broadcast_to(duals[None], (Z * Y, JB_DEV, BLOCK))
    rows = lax.all_to_all(copies, ("z", "y"), split_axis=0, concat_axis=0, tiled=True)
    rows = lax.all_gather(rows.reshape(Z * Y * JB_DEV, BLOCK), "c", axis=0, tiled=True)
    primal, send, member = pl.pallas_call(
        allocate_kernel,
        out_shape=(
            jax.ShapeDtypeStruct((CAP, BLOCK, BLOCK), jnp.bfloat16),
            jax.ShapeDtypeStruct((MEM * ROWS, BLOCK), jnp.float32),
            jax.ShapeDtypeStruct((MB_DEV, BLOCK), jnp.float32),
        ),
        in_specs=[smem, smem, smem, vmem, vmem, vmem],
        out_specs=(vmem, vmem, vmem),
        scratch_shapes=[pltpu.SMEM((MEM,), jnp.int32)],
        compiler_params=pltpu.CompilerParams(vmem_limit_bytes=16 * 1024 * 1024),
        cost_estimate=pl.CostEstimate(flops=8 * CAP * BLOCK * BLOCK, bytes_accessed=6 * CAP * BLOCK * BLOCK, transcendentals=0),
        name="allocate",
    )(slot_owner.reshape(1, CAP), slot_local, slot_member, rows, pair_cost, pair_coef)
    others = [lax.ppermute(member, "x", [(i, i ^ k) for i in range(X)]) for k in (1, 2, 3)]
    recv = lax.all_to_all(
        send.reshape(MEM, ROWS, BLOCK), ("z", "y", "c"), split_axis=0, concat_axis=0, tiled=True
    ).reshape(MEM * ROWS, BLOCK)
    gradient, share = pl.pallas_call(
        finish_kernel,
        out_shape=(
            jax.ShapeDtypeStruct((JB_DEV, BLOCK), jnp.float32),
            jax.ShapeDtypeStruct((MB_DEV, BLOCK), jnp.float32),
        ),
        in_specs=[vmem] * 6,
        out_specs=(vmem, vmem),
        name="finish",
    )(recv, member, *others, capacity)
    return primal, gradient, share


def solution(mesh):
    axes = ("z", "y", "c", "x")
    fine = Mesh(mesh.devices.reshape(Z, Y, C, X), axes)
    each = lambda n: P(axes, *([None] * (n - 1)))
    return jax.shard_map(
        per_device,
        mesh=fine,
        in_specs=(each(3), each(3), each(2), each(3), each(2), each(2), each(2)),
        out_specs=(each(3), each(2), P(("z", "y", "c"), None)),
        check_vma=False,
    )
```

```python
import jax
import jax.numpy as jnp
from jax import lax
from jax.experimental import pallas as pl
from jax.experimental.pallas import tpu as pltpu
from jax.sharding import Mesh, PartitionSpec as P

Z, Y, C, X = 8, 4, 2, 4
CAP = 48
BLOCK = 128
MB_DEV = 32
JB_DEV = 16
MEM = Z * Y * C
ROWS = 4
EARLY = 24
LATE = CAP - EARLY
HALF = Z * Y * JB_DEV
LOCAL, MEMBER, ROW, OTHER, PLACE = (i * CAP for i in range(5))
VMEM = pl.BlockSpec(memory_space=pltpu.VMEM)
SMEM = pl.BlockSpec(memory_space=pltpu.SMEM)
ANY = pl.BlockSpec(memory_space=pl.ANY)


def in_hbm(a):
    return pltpu.with_memory_space_constraint(a, pltpu.HBM)


def in_vmem(a):
    return pltpu.with_memory_space_constraint(a, pltpu.VMEM)


def stage_kernel(
    owner_ref, local_in_ref, member_in_ref, cost_in_ref, coef_in_ref,
    cost_ref, coef_ref, number_ref, count_ref, sem,
):
    load_cost = pltpu.make_async_copy(cost_in_ref.at[pl.ds(0, EARLY)], cost_ref, sem.at[0])
    load_coef = pltpu.make_async_copy(coef_in_ref.at[pl.ds(0, EARLY)], coef_ref, sem.at[1])
    load_cost.start()
    load_coef.start()
    core = lax.axis_index("c")

    def clear(i, carry):
        count_ref[i] = 0
        return carry

    lax.fori_loop(0, MEM, clear, 0)

    def slot(s, carry):
        owner = owner_ref[0, s]
        local = local_in_ref[0, s]
        number_ref[LOCAL + s] = local
        number_ref[MEMBER + s] = member_in_ref[0, s]
        number_ref[ROW + s] = (owner >> 1) * JB_DEV + local
        number_ref[OTHER + s] = (owner & 1) ^ core
        k = count_ref[owner]
        count_ref[owner] = k + 1
        number_ref[PLACE + s] = owner * ROWS + k
        return carry

    lax.fori_loop(0, CAP, slot, 0)
    load_cost.wait()
    load_coef.wait()


def stage_late_kernel(cost_in_ref, coef_in_ref, cost_ref, coef_ref, sem):
    load_cost = pltpu.make_async_copy(cost_in_ref.at[pl.ds(EARLY, LATE)], cost_ref, sem.at[0])
    load_coef = pltpu.make_async_copy(coef_in_ref.at[pl.ds(EARLY, LATE)], coef_ref, sem.at[1])
    load_cost.start()
    load_coef.start()
    load_cost.wait()
    load_coef.wait()


def allocate_kernel(
    number_ref, own_rows_ref, other_rows_ref,
    early_cost_ref, early_coef_ref, late_cost_ref, late_coef_ref,
    primal_ref, send_ref, member_out_ref, slot_ref, column_ref, sums_ref,
):
    send_ref[...] = jnp.full((MEM * ROWS, BLOCK), -1.0, jnp.float32)
    member_out_ref[...] = jnp.zeros((MB_DEV, BLOCK), jnp.float32)
    for s in range(CAP):
        at = pl.ds(number_ref[ROW + s], 1)
        slot_ref[s:s + 1, :] = -jnp.where(number_ref[OTHER + s] == 1, other_rows_ref[at, :], own_rows_ref[at, :])
    ones = jnp.ones((8, 2 * BLOCK), jnp.bfloat16)

    def block(s, cost_ref, coef_ref, at):
        minus_dual = slot_ref[pl.ds(s, 1), :]
        column, parts = None, []
        for g in range(0, BLOCK, 32):
            cost = cost_ref[at, g:g + 32].astype(jnp.float32)
            coef = coef_ref[at, g:g + 32].astype(jnp.float32)
            alloc = jnp.minimum(jnp.maximum(coef * minus_dual - cost, 0.0), 1.0)
            high = alloc.astype(jnp.bfloat16)
            primal_ref[s, g:g + 32] = high
            rest = (alloc - high.astype(jnp.float32)).astype(jnp.bfloat16)
            parts.append(jnp.concatenate([high, rest], axis=1))
            part = jnp.sum((coef * alloc).reshape(4, 8, BLOCK), axis=0)
            column = part if column is None else column + part
        column_ref[pl.ds(pl.multiple_of(s * 8, 8), 8), :] = column
        return parts

    def run(first, count, cost_ref, coef_ref, unroll):
        def pair(i, carry):
            s = first + 2 * i
            parts = block(s, cost_ref, coef_ref, 2 * i) + block(s + 1, cost_ref, coef_ref, 2 * i + 1)
            both = jnp.concatenate(parts, axis=0)
            sums = lax.dot_general(ones, both, (((1,), (1,)), ((), ())), preferred_element_type=jnp.float32)
            sums_ref[pl.ds(s, 1), :] = sums[0:1, :BLOCK]
            sums_ref[pl.ds(s + 1, 1), :] = sums[0:1, BLOCK:]
            return carry

        lax.fori_loop(0, count // 2, pair, 0, unroll=unroll)

    run(0, EARLY, early_cost_ref, early_coef_ref, 12)
    run(EARLY, LATE, late_cost_ref, late_coef_ref, 12)
    slot_ref[...] = jnp.sum(column_ref[...].reshape(CAP, 8, BLOCK), axis=1)
    for s in range(CAP):
        place = number_ref[PLACE + s]
        send_ref[pl.ds(place, 1), :] = slot_ref[s:s + 1, :]
        send_ref[pl.ds(place + 2, 1), :] = jnp.full((1, BLOCK), number_ref[LOCAL + s].astype(jnp.float32))
        member_out_ref[pl.ds(number_ref[MEMBER + s], 1), :] += sums_ref[s:s + 1, :]


def finish_kernel(recv_ref, m0_ref, m1_ref, m2_ref, m3_ref, capacity_ref, gradient_ref, share_ref):
    share_ref[...] = ((m0_ref[...] + m1_ref[...]) + (m2_ref[...] + m3_ref[...])) * (1.0 / BLOCK)
    sub = lax.broadcasted_iota(jnp.int32, (8, BLOCK), 0) % 4
    data = sub < 2
    totals = [jnp.zeros((8, BLOCK), jnp.float32) for _ in range(JB_DEV)]
    for i in range(MEM * ROWS // 8):
        got = recv_ref[i * 8:(i + 1) * 8, :]
        name = jnp.where(data, pltpu.roll(got, 6, 0), -1.0)
        for k in range(JB_DEV):
            totals[k] = totals[k] + jnp.where(name == float(k), got, 0.0)
    summed = jnp.concatenate([jnp.sum(t, axis=0, keepdims=True) for t in totals], axis=0)
    gradient_ref[...] = summed - capacity_ref[...].astype(jnp.float32)


def stage(owner, local, member, cost, coef):
    early = pltpu.VMEM((EARLY, BLOCK, BLOCK), jnp.bfloat16)
    return pl.pallas_call(
        stage_kernel,
        out_shape=(early, early, jax.ShapeDtypeStruct((5 * CAP,), jnp.int32)),
        in_specs=[SMEM] * 3 + [ANY] * 2,
        out_specs=(VMEM, VMEM, SMEM),
        scratch_shapes=[pltpu.SMEM((MEM,), jnp.int32), pltpu.SemaphoreType.DMA((2,))],
        compiler_params=pltpu.CompilerParams(vmem_limit_bytes=4 * 1024 * 1024),
        cost_estimate=pl.CostEstimate(flops=0, bytes_accessed=8 * EARLY * BLOCK * BLOCK, transcendentals=0),
        name="stage",
    )(owner, local, member, in_hbm(cost), in_hbm(coef))


def stage_late(cost, coef):
    late = pltpu.VMEM((LATE, BLOCK, BLOCK), jnp.bfloat16)
    return pl.pallas_call(
        stage_late_kernel,
        out_shape=(late, late),
        in_specs=[ANY] * 2,
        out_specs=(VMEM, VMEM),
        scratch_shapes=[pltpu.SemaphoreType.DMA((2,))],
        compiler_params=pltpu.CompilerParams(vmem_limit_bytes=4 * 1024 * 1024),
        cost_estimate=pl.CostEstimate(flops=0, bytes_accessed=8 * LATE * BLOCK * BLOCK, transcendentals=0),
        name="stage_late",
    )(in_hbm(cost), in_hbm(coef))


def allocate(number, *blocks):
    return pl.pallas_call(
        allocate_kernel,
        out_shape=(
            pltpu.VMEM((CAP, BLOCK, BLOCK), jnp.bfloat16),
            jax.ShapeDtypeStruct((MEM * ROWS, BLOCK), jnp.float32),
            pltpu.VMEM((MB_DEV, BLOCK), jnp.float32),
        ),
        in_specs=[SMEM] + [VMEM] * 6,
        out_specs=(VMEM, VMEM, VMEM),
        scratch_shapes=[
            pltpu.VMEM((CAP, BLOCK), jnp.float32),
            pltpu.VMEM((CAP * 8, BLOCK), jnp.float32),
            pltpu.VMEM((CAP, BLOCK), jnp.float32),
        ],
        compiler_params=pltpu.CompilerParams(vmem_limit_bytes=8 * 1024 * 1024),
        cost_estimate=pl.CostEstimate(
            flops=8 * CAP * BLOCK * BLOCK, bytes_accessed=6 * CAP * BLOCK * BLOCK, transcendentals=0
        ),
        name="allocate",
    )(number, *map(in_vmem, blocks))


def finish(recv, share, others, capacity):
    return pl.pallas_call(
        finish_kernel,
        out_shape=(
            jax.ShapeDtypeStruct((JB_DEV, BLOCK), jnp.float32),
            jax.ShapeDtypeStruct((MB_DEV, BLOCK), jnp.float32),
        ),
        in_specs=[VMEM] * 6,
        out_specs=(VMEM, VMEM),
        compiler_params=pltpu.CompilerParams(vmem_limit_bytes=2 * 1024 * 1024),
        name="finish",
    )(recv, share, *others, capacity)


def per_device(pair_cost, pair_coef, slot_member, slot_owner, slot_local, duals, capacity):
    copies = jnp.broadcast_to(duals[None], (Z * Y, JB_DEV, BLOCK))
    rows = lax.all_to_all(copies, ("z", "y"), split_axis=0, concat_axis=0, tiled=True).reshape(HALF, BLOCK)
    cost, coef, number = stage(
        slot_owner.reshape(1, CAP), slot_local, slot_member, pair_cost, pair_coef
    )
    rows, number, late_cost, late_coef = lax.optimization_barrier((rows, number, pair_cost, pair_coef))
    other_rows = lax.ppermute(rows, "c", [(0, 1), (1, 0)])
    late_cost, late_coef = stage_late(late_cost, late_coef)
    primal, send, share = allocate(number, rows, other_rows, cost, coef, late_cost, late_coef)
    others = [lax.ppermute(share, "x", [(i, i ^ k) for i in range(X)]) for k in (1, 2, 3)]
    recv = lax.all_to_all(
        send.reshape(MEM, ROWS, BLOCK), ("z", "y", "c"), split_axis=0, concat_axis=0, tiled=True
    ).reshape(MEM * ROWS, BLOCK)
    gradient, share = finish(recv, share, others, capacity)
    return primal, gradient, share


def solution(mesh):
    axes = ("z", "y", "c", "x")
    fine = Mesh(mesh.devices.reshape(Z, Y, C, X), axes)
    each = lambda n: P(axes, *([None] * (n - 1)))
    return jax.shard_map(
        per_device,
        mesh=fine,
        in_specs=(each(3), each(3), each(2), each(3), each(2), each(2), each(2)),
        out_specs=(each(3), each(2), P(("z", "y", "c"), None)),
        check_vma=False,
    )
```

```python
import jax
import jax.numpy as jnp
from jax import lax
from jax.experimental import pallas as pl
from jax.experimental.pallas import tpu as pltpu
from jax.sharding import Mesh, PartitionSpec as P

Z, Y, C, X = 8, 4, 2, 4
CAP = 48
BLOCK = 128
MB_DEV = 32
JB_DEV = 16
MEM = Z * Y * C
ROWS = 3
MIB = 1024 * 1024
EARLY = 24
LATE = CAP - EARLY
HALF = Z * Y * JB_DEV
MEMBER, ROW, OTHER, PLACE = (i * CAP for i in range(4))
VMEM = pl.BlockSpec(memory_space=pltpu.VMEM)
SMEM = pl.BlockSpec(memory_space=pltpu.SMEM)
ANY = pl.BlockSpec(memory_space=pl.ANY)


def in_hbm(a):
    return pltpu.with_memory_space_constraint(a, pltpu.HBM)


def in_vmem(a):
    return pltpu.with_memory_space_constraint(a, pltpu.VMEM)


def spread_kernel(duals_ref, out_ref, one_ref, many_ref, sem):
    load = pltpu.make_async_copy(duals_ref, one_ref, sem.at[0])
    load.start()
    load.wait()
    many_ref[...] = jnp.broadcast_to(one_ref[...][None], many_ref.shape)
    store = pltpu.make_async_copy(many_ref, out_ref, sem.at[1])
    store.start()
    store.wait()


def spread(duals):
    copies = (Z * Y, JB_DEV, BLOCK)
    return pl.pallas_call(
        spread_kernel,
        out_shape=jax.ShapeDtypeStruct(copies, jnp.float32),
        in_specs=[ANY],
        out_specs=ANY,
        scratch_shapes=[
            pltpu.VMEM((JB_DEV, BLOCK), jnp.float32),
            pltpu.VMEM(copies, jnp.float32),
            pltpu.SemaphoreType.DMA((2,)),
        ],
        compiler_params=pltpu.CompilerParams(vmem_limit_bytes=2 * MIB),
        name="spread",
    )(in_hbm(duals))


def stage_kernel(
    owner_ref, local_in_ref, member_in_ref, cost_in_ref, coef_in_ref,
    cost_ref, coef_ref, named_ref, number_ref, count_ref, sem,
):
    load_cost = pltpu.make_async_copy(cost_in_ref.at[pl.ds(0, EARLY)], cost_ref, sem.at[0])
    load_coef = pltpu.make_async_copy(coef_in_ref.at[pl.ds(0, EARLY)], coef_ref, sem.at[1])
    load_cost.start()
    load_coef.start()
    core = lax.axis_index("c")
    lane = lax.broadcasted_iota(jnp.int32, (1, BLOCK), 1)
    named_ref[...] = jnp.full((MEM, 1, BLOCK), -1.0, jnp.float32)

    def clear(i, carry):
        count_ref[i] = 0
        return carry

    lax.fori_loop(0, MEM, clear, 0)

    def slot(s, carry):
        owner = owner_ref[0, s]
        local = local_in_ref[0, s]
        number_ref[MEMBER + s] = member_in_ref[0, s]
        number_ref[ROW + s] = (owner >> 1) * JB_DEV + local
        number_ref[OTHER + s] = (owner & 1) ^ core
        k = count_ref[owner]
        count_ref[owner] = k + 1
        number_ref[PLACE + s] = owner * ROWS + k
        half = (lane >= BLOCK // 2) == (k == 1)
        named_ref[owner] = jnp.where(half, local.astype(jnp.float32), named_ref[owner])
        return carry

    lax.fori_loop(0, CAP, slot, 0)
    load_cost.wait()
    load_coef.wait()


def stage_late_kernel(cost_in_ref, coef_in_ref, cost_ref, coef_ref, sem):
    load_cost = pltpu.make_async_copy(cost_in_ref.at[pl.ds(EARLY, LATE)], cost_ref, sem.at[0])
    load_coef = pltpu.make_async_copy(coef_in_ref.at[pl.ds(EARLY, LATE)], coef_ref, sem.at[1])
    load_cost.start()
    load_coef.start()
    load_cost.wait()
    load_coef.wait()


def allocate_kernel(
    number_ref, named_ref, own_rows_ref, other_rows_ref,
    early_cost_ref, early_coef_ref, late_cost_ref, late_coef_ref,
    primal_ref, send_ref, member_out_ref, slot_ref, column_ref, sums_ref,
):
    send_ref[...] = jnp.zeros((MEM * ROWS, 1, BLOCK), jnp.float32)
    for i in range(MEM):
        send_ref[i * ROWS + 2] = named_ref[i]
    member_out_ref[...] = jnp.zeros((MB_DEV, BLOCK), jnp.float32)
    for s in range(CAP):
        at = pl.ds(number_ref[ROW + s], 1)
        slot_ref[s:s + 1, :] = -jnp.where(number_ref[OTHER + s] == 1, other_rows_ref[at, :], own_rows_ref[at, :])
    ones = jnp.ones((8, 2 * BLOCK), jnp.bfloat16)

    def block(s, cost_ref, coef_ref, at):
        minus_dual = slot_ref[pl.ds(s, 1), :]
        column, parts = None, []
        for g in range(0, BLOCK, 32):
            cost = cost_ref[at, g:g + 32].astype(jnp.float32)
            coef = coef_ref[at, g:g + 32].astype(jnp.float32)
            alloc = jnp.minimum(jnp.maximum(coef * minus_dual - cost, 0.0), 1.0)
            high = alloc.astype(jnp.bfloat16)
            primal_ref[s, g:g + 32] = high
            rest = (alloc - high.astype(jnp.float32)).astype(jnp.bfloat16)
            parts.append(jnp.concatenate([high, rest], axis=1))
            part = jnp.sum((coef * alloc).reshape(4, 8, BLOCK), axis=0)
            column = part if column is None else column + part
        column_ref[pl.ds(pl.multiple_of(s * 8, 8), 8), :] = column
        return parts

    def run(first, count, cost_ref, coef_ref, unroll):
        def pair(i, carry):
            s = first + 2 * i
            parts = block(s, cost_ref, coef_ref, 2 * i) + block(s + 1, cost_ref, coef_ref, 2 * i + 1)
            both = jnp.concatenate(parts, axis=0)
            sums = lax.dot_general(ones, both, (((1,), (1,)), ((), ())), preferred_element_type=jnp.float32)
            sums_ref[pl.ds(s, 1), :] = sums[0:1, :BLOCK]
            sums_ref[pl.ds(s + 1, 1), :] = sums[0:1, BLOCK:]
            return carry

        lax.fori_loop(0, count // 2, pair, 0, unroll=unroll)

    run(0, EARLY, early_cost_ref, early_coef_ref, 12)
    run(EARLY, LATE, late_cost_ref, late_coef_ref, 12)
    slot_ref[...] = jnp.sum(column_ref[...].reshape(CAP, 8, BLOCK), axis=1)
    for s in range(CAP):
        send_ref[number_ref[PLACE + s]] = slot_ref[s:s + 1, :]
        member_out_ref[pl.ds(number_ref[MEMBER + s], 1), :] += sums_ref[s:s + 1, :]


def finish_kernel(recv_ref, m0_ref, m1_ref, m2_ref, m3_ref, capacity_ref, gradient_ref, share_ref):
    share_ref[...] = ((m0_ref[...] + m1_ref[...]) + (m2_ref[...] + m3_ref[...])) * (1.0 / BLOCK)
    low = lax.broadcasted_iota(jnp.int32, (8, BLOCK), 1) < BLOCK // 2
    totals = [jnp.zeros((8, BLOCK), jnp.float32) for _ in range(JB_DEV)]
    for i in range(0, MEM, 8):
        first, second, named = (recv_ref[i:i + 8, 0, j * BLOCK:(j + 1) * BLOCK] for j in range(ROWS))
        turned = pltpu.roll(named, BLOCK // 2, 1)
        name_first = jnp.where(low, named, turned)
        name_second = jnp.where(low, turned, named)
        for k in range(JB_DEV):
            totals[k] = totals[k] + jnp.where(name_first == float(k), first, 0.0)
            totals[k] = totals[k] + jnp.where(name_second == float(k), second, 0.0)
    summed = jnp.concatenate([jnp.sum(t, axis=0, keepdims=True) for t in totals], axis=0)
    gradient_ref[...] = summed - capacity_ref[...].astype(jnp.float32)


def stage(owner, local, member, cost, coef):
    early = pltpu.VMEM((EARLY, BLOCK, BLOCK), jnp.bfloat16)
    return pl.pallas_call(
        stage_kernel,
        out_shape=(
            early,
            early,
            pltpu.VMEM((MEM, 1, BLOCK), jnp.float32),
            jax.ShapeDtypeStruct((4 * CAP,), jnp.int32),
        ),
        in_specs=[SMEM] * 3 + [ANY] * 2,
        out_specs=(VMEM, VMEM, VMEM, SMEM),
        scratch_shapes=[pltpu.SMEM((MEM,), jnp.int32), pltpu.SemaphoreType.DMA((2,))],
        compiler_params=pltpu.CompilerParams(vmem_limit_bytes=4 * 1024 * 1024),
        cost_estimate=pl.CostEstimate(flops=0, bytes_accessed=8 * EARLY * BLOCK * BLOCK, transcendentals=0),
        name="stage",
    )(owner, local, member, in_hbm(cost), in_hbm(coef))


def stage_late(cost, coef):
    late = pltpu.VMEM((LATE, BLOCK, BLOCK), jnp.bfloat16)
    return pl.pallas_call(
        stage_late_kernel,
        out_shape=(late, late),
        in_specs=[ANY] * 2,
        out_specs=(VMEM, VMEM),
        scratch_shapes=[pltpu.SemaphoreType.DMA((2,))],
        compiler_params=pltpu.CompilerParams(vmem_limit_bytes=4 * 1024 * 1024),
        cost_estimate=pl.CostEstimate(flops=0, bytes_accessed=8 * LATE * BLOCK * BLOCK, transcendentals=0),
        name="stage_late",
    )(in_hbm(cost), in_hbm(coef))


def allocate(number, *blocks):
    return pl.pallas_call(
        allocate_kernel,
        out_shape=(
            pltpu.VMEM((CAP, BLOCK, BLOCK), jnp.bfloat16),
            jax.ShapeDtypeStruct((MEM * ROWS, 1, BLOCK), jnp.float32),
            pltpu.VMEM((MB_DEV, BLOCK), jnp.float32),
        ),
        in_specs=[SMEM] + [VMEM] * 7,
        out_specs=(VMEM, VMEM, VMEM),
        scratch_shapes=[
            pltpu.VMEM((CAP, BLOCK), jnp.float32),
            pltpu.VMEM((CAP * 8, BLOCK), jnp.float32),
            pltpu.VMEM((CAP, BLOCK), jnp.float32),
        ],
        compiler_params=pltpu.CompilerParams(vmem_limit_bytes=8 * 1024 * 1024),
        cost_estimate=pl.CostEstimate(
            flops=8 * CAP * BLOCK * BLOCK, bytes_accessed=6 * CAP * BLOCK * BLOCK, transcendentals=0
        ),
        name="allocate",
    )(number, *map(in_vmem, blocks))


def finish(recv, share, others, capacity):
    return pl.pallas_call(
        finish_kernel,
        out_shape=(
            jax.ShapeDtypeStruct((JB_DEV, BLOCK), jnp.float32),
            jax.ShapeDtypeStruct((MB_DEV, BLOCK), jnp.float32),
        ),
        in_specs=[VMEM] * 6,
        out_specs=(VMEM, VMEM),
        compiler_params=pltpu.CompilerParams(vmem_limit_bytes=2 * 1024 * 1024),
        name="finish",
    )(recv, share, *others, capacity)


def per_device(pair_cost, pair_coef, slot_member, slot_owner, slot_local, duals, capacity):
    copies = spread(duals)
    rows = lax.all_to_all(copies, ("z", "y"), split_axis=0, concat_axis=0, tiled=True).reshape(HALF, BLOCK)
    cost, coef, named, number = stage(
        slot_owner.reshape(1, CAP), slot_local, slot_member, pair_cost, pair_coef
    )
    rows, number, late_cost, late_coef = lax.optimization_barrier((rows, number, pair_cost, pair_coef))
    other_rows = lax.ppermute(rows, "c", [(0, 1), (1, 0)])
    late_cost, late_coef = stage_late(late_cost, late_coef)
    primal, send, share = allocate(number, named, rows, other_rows, cost, coef, late_cost, late_coef)
    others = [lax.ppermute(share, "x", [(i, i ^ k) for i in range(X)]) for k in (1, 2, 3)]
    send = send.reshape(MEM, 1, ROWS * BLOCK)
    recv = lax.all_to_all(send, ("z", "y", "c"), split_axis=0, concat_axis=0, tiled=True)
    gradient, share = finish(recv, share, others, capacity)
    return primal, gradient, share


def solution(mesh):
    axes = ("z", "y", "c", "x")
    fine = Mesh(mesh.devices.reshape(Z, Y, C, X), axes)
    each = lambda n: P(axes, *([None] * (n - 1)))
    return jax.shard_map(
        per_device,
        mesh=fine,
        in_specs=(each(3), each(3), each(2), each(3), each(2), each(2), each(2)),
        out_specs=(each(3), each(2), P(("z", "y", "c"), None)),
        check_vma=False,
    )
```

```python
import jax
import jax.numpy as jnp
from jax import lax
from jax.experimental import pallas as pl
from jax.experimental.pallas import tpu as pltpu
from jax.sharding import Mesh, PartitionSpec as P

Z, Y, C, X = 8, 4, 2, 4
CAP = 48
BLOCK = 128
MB_DEV = 32
JB_DEV = 16
MEM = Z * Y * C
ROWS = 3
MIB = 1024 * 1024
EARLY = 24
LATE = CAP - EARLY
CHUNKS = 3
PER = CAP // CHUNKS
HALF = Z * Y * JB_DEV
MEMBER, ROW, OTHER, PLACE = (i * CAP for i in range(4))
VMEM = pl.BlockSpec(memory_space=pltpu.VMEM)
SMEM = pl.BlockSpec(memory_space=pltpu.SMEM)
ANY = pl.BlockSpec(memory_space=pl.ANY)


def in_hbm(a):
    return pltpu.with_memory_space_constraint(a, pltpu.HBM)


def in_vmem(a):
    return pltpu.with_memory_space_constraint(a, pltpu.VMEM)


def spread_kernel(duals_ref, out_ref, one_ref, many_ref, sem):
    load = pltpu.make_async_copy(duals_ref, one_ref, sem.at[0])
    load.start()
    load.wait()
    many_ref[...] = jnp.broadcast_to(one_ref[...][None], many_ref.shape)
    store = pltpu.make_async_copy(many_ref, out_ref, sem.at[1])
    store.start()
    store.wait()


def spread(duals):
    copies = (Z * Y, JB_DEV, BLOCK)
    return pl.pallas_call(
        spread_kernel,
        out_shape=jax.ShapeDtypeStruct(copies, jnp.float32),
        in_specs=[ANY],
        out_specs=ANY,
        scratch_shapes=[
            pltpu.VMEM((JB_DEV, BLOCK), jnp.float32),
            pltpu.VMEM(copies, jnp.float32),
            pltpu.SemaphoreType.DMA((2,)),
        ],
        compiler_params=pltpu.CompilerParams(vmem_limit_bytes=2 * MIB),
        name="spread",
    )(in_hbm(duals))


def stage_kernel(
    owner_ref, local_in_ref, member_in_ref, cost_in_ref, coef_in_ref,
    cost_ref, coef_ref, named_ref, number_ref, count_ref, sem,
):
    load_cost = pltpu.make_async_copy(cost_in_ref.at[pl.ds(0, EARLY)], cost_ref, sem.at[0])
    load_coef = pltpu.make_async_copy(coef_in_ref.at[pl.ds(0, EARLY)], coef_ref, sem.at[1])
    load_cost.start()
    load_coef.start()
    core = lax.axis_index("c")
    lane = lax.broadcasted_iota(jnp.int32, (1, BLOCK), 1)
    named_ref[...] = jnp.full((MEM, 1, BLOCK), -1.0, jnp.float32)

    def clear(i, carry):
        count_ref[i] = 0
        return carry

    lax.fori_loop(0, MEM, clear, 0)

    def slot(s, carry):
        owner = owner_ref[0, s]
        local = local_in_ref[0, s]
        number_ref[MEMBER + s] = member_in_ref[0, s]
        number_ref[ROW + s] = (owner >> 1) * JB_DEV + local
        number_ref[OTHER + s] = (owner & 1) ^ core
        k = count_ref[owner]
        count_ref[owner] = k + 1
        number_ref[PLACE + s] = owner * ROWS + k
        half = (lane >= BLOCK // 2) == (k == 1)
        named_ref[owner] = jnp.where(half, local.astype(jnp.float32), named_ref[owner])
        return carry

    lax.fori_loop(0, CAP, slot, 0)
    load_cost.wait()
    load_coef.wait()


def stage_late_kernel(cost_in_ref, coef_in_ref, cost_ref, coef_ref, sem):
    load_cost = pltpu.make_async_copy(cost_in_ref.at[pl.ds(EARLY, LATE)], cost_ref, sem.at[0])
    load_coef = pltpu.make_async_copy(coef_in_ref.at[pl.ds(EARLY, LATE)], coef_ref, sem.at[1])
    load_cost.start()
    load_coef.start()
    load_cost.wait()
    load_coef.wait()


def columns_kernel(
    number_ref, named_ref, own_rows_ref, other_rows_ref,
    early_cost_ref, early_coef_ref, late_cost_ref, late_coef_ref,
    send_ref, minus_ref, column_ref, total_ref,
):
    send_ref[...] = jnp.zeros((MEM * ROWS, 1, BLOCK), jnp.float32)
    for i in range(MEM):
        send_ref[i * ROWS + 2] = named_ref[i]
    for s in range(CAP):
        at = pl.ds(number_ref[ROW + s], 1)
        minus_ref[s:s + 1, :] = -jnp.where(number_ref[OTHER + s] == 1, other_rows_ref[at, :], own_rows_ref[at, :])

    def run(first, count, cost_ref, coef_ref):
        def block(i, carry):
            s = first + i
            minus_dual = minus_ref[pl.ds(s, 1), :]
            column = None
            for g in range(0, BLOCK, 32):
                cost = cost_ref[i, g:g + 32].astype(jnp.float32)
                coef = coef_ref[i, g:g + 32].astype(jnp.float32)
                alloc = jnp.minimum(jnp.maximum(coef * minus_dual - cost, 0.0), 1.0)
                part = jnp.sum((coef * alloc).reshape(4, 8, BLOCK), axis=0)
                column = part if column is None else column + part
            column_ref[pl.ds(pl.multiple_of(s * 8, 8), 8), :] = column
            return carry

        lax.fori_loop(0, count, block, 0, unroll=count)

    run(0, EARLY, early_cost_ref, early_coef_ref)
    run(EARLY, LATE, late_cost_ref, late_coef_ref)
    total_ref[...] = jnp.sum(column_ref[...].reshape(CAP, 8, BLOCK), axis=1)
    for s in range(CAP):
        send_ref[number_ref[PLACE + s]] = total_ref[s:s + 1, :]


def primal_kernel(
    number_ref, minus_ref, cost_in_ref, coef_in_ref,
    primal_out_ref, member_out_ref, cost_ref, coef_ref, primal_ref, sums_ref, in_sem, out_sem,
):
    def loads(k):
        part = pl.ds(k * PER, PER)
        return (
            pltpu.make_async_copy(cost_in_ref.at[part], cost_ref.at[part], in_sem.at[0, k]),
            pltpu.make_async_copy(coef_in_ref.at[part], coef_ref.at[part], in_sem.at[1, k]),
        )

    def leave(k):
        part = pl.ds(k * PER, PER)
        return pltpu.make_async_copy(primal_ref.at[part], primal_out_ref.at[part], out_sem.at[k])

    for k in range(CHUNKS):
        for load in loads(k):
            load.start()
    member_out_ref[...] = jnp.zeros((MB_DEV, BLOCK), jnp.float32)
    ones = jnp.ones((8, 2 * BLOCK), jnp.bfloat16)

    def block(s):
        minus_dual = minus_ref[pl.ds(s, 1), :]
        parts = []
        for g in range(0, BLOCK, 32):
            cost = cost_ref[s, g:g + 32].astype(jnp.float32)
            coef = coef_ref[s, g:g + 32].astype(jnp.float32)
            alloc = jnp.minimum(jnp.maximum(coef * minus_dual - cost, 0.0), 1.0)
            high = alloc.astype(jnp.bfloat16)
            primal_ref[s, g:g + 32] = high
            rest = (alloc - high.astype(jnp.float32)).astype(jnp.bfloat16)
            parts.append(jnp.concatenate([high, rest], axis=1))
        return parts

    for k in range(CHUNKS):
        for load in loads(k):
            load.wait()

        def pair(i, carry):
            s = k * PER + 2 * i
            both = jnp.concatenate(block(s) + block(s + 1), axis=0)
            sums = lax.dot_general(ones, both, (((1,), (1,)), ((), ())), preferred_element_type=jnp.float32)
            sums_ref[pl.ds(s, 1), :] = sums[0:1, :BLOCK]
            sums_ref[pl.ds(s + 1, 1), :] = sums[0:1, BLOCK:]
            return carry

        lax.fori_loop(0, PER // 2, pair, 0, unroll=PER // 2)
        leave(k).start()
    for s in range(CAP):
        member_out_ref[pl.ds(number_ref[MEMBER + s], 1), :] += sums_ref[s:s + 1, :]
    for k in range(CHUNKS):
        leave(k).wait()


def finish_kernel(recv_ref, m0_ref, m1_ref, m2_ref, m3_ref, capacity_ref, gradient_ref, share_ref):
    share_ref[...] = ((m0_ref[...] + m1_ref[...]) + (m2_ref[...] + m3_ref[...])) * (1.0 / BLOCK)
    low = lax.broadcasted_iota(jnp.int32, (8, BLOCK), 1) < BLOCK // 2
    totals = [jnp.zeros((8, BLOCK), jnp.float32) for _ in range(JB_DEV)]
    for i in range(0, MEM, 8):
        first, second, named = (recv_ref[i:i + 8, 0, j * BLOCK:(j + 1) * BLOCK] for j in range(ROWS))
        turned = pltpu.roll(named, BLOCK // 2, 1)
        name_first = jnp.where(low, named, turned)
        name_second = jnp.where(low, turned, named)
        for k in range(JB_DEV):
            totals[k] = totals[k] + jnp.where(name_first == float(k), first, 0.0)
            totals[k] = totals[k] + jnp.where(name_second == float(k), second, 0.0)
    summed = jnp.concatenate([jnp.sum(t, axis=0, keepdims=True) for t in totals], axis=0)
    gradient_ref[...] = summed - capacity_ref[...].astype(jnp.float32)


def stage(owner, local, member, cost, coef):
    early = pltpu.VMEM((EARLY, BLOCK, BLOCK), jnp.bfloat16)
    return pl.pallas_call(
        stage_kernel,
        out_shape=(
            early,
            early,
            pltpu.VMEM((MEM, 1, BLOCK), jnp.float32),
            jax.ShapeDtypeStruct((4 * CAP,), jnp.int32),
        ),
        in_specs=[SMEM] * 3 + [ANY] * 2,
        out_specs=(VMEM, VMEM, VMEM, SMEM),
        scratch_shapes=[pltpu.SMEM((MEM,), jnp.int32), pltpu.SemaphoreType.DMA((2,))],
        compiler_params=pltpu.CompilerParams(vmem_limit_bytes=4 * 1024 * 1024),
        cost_estimate=pl.CostEstimate(flops=0, bytes_accessed=8 * EARLY * BLOCK * BLOCK, transcendentals=0),
        name="stage",
    )(owner, local, member, in_hbm(cost), in_hbm(coef))


def stage_late(cost, coef):
    late = pltpu.VMEM((LATE, BLOCK, BLOCK), jnp.bfloat16)
    return pl.pallas_call(
        stage_late_kernel,
        out_shape=(late, late),
        in_specs=[ANY] * 2,
        out_specs=(VMEM, VMEM),
        scratch_shapes=[pltpu.SemaphoreType.DMA((2,))],
        compiler_params=pltpu.CompilerParams(vmem_limit_bytes=4 * 1024 * 1024),
        cost_estimate=pl.CostEstimate(flops=0, bytes_accessed=8 * LATE * BLOCK * BLOCK, transcendentals=0),
        name="stage_late",
    )(in_hbm(cost), in_hbm(coef))


def columns(number, *blocks):
    return pl.pallas_call(
        columns_kernel,
        out_shape=(
            jax.ShapeDtypeStruct((MEM * ROWS, 1, BLOCK), jnp.float32),
            pltpu.VMEM((CAP, BLOCK), jnp.float32),
        ),
        in_specs=[SMEM] + [VMEM] * 7,
        out_specs=(VMEM, VMEM),
        scratch_shapes=[pltpu.VMEM((CAP * 8, BLOCK), jnp.float32), pltpu.VMEM((CAP, BLOCK), jnp.float32)],
        compiler_params=pltpu.CompilerParams(vmem_limit_bytes=8 * MIB),
        cost_estimate=pl.CostEstimate(
            flops=6 * CAP * BLOCK * BLOCK, bytes_accessed=4 * CAP * BLOCK * BLOCK, transcendentals=0
        ),
        name="columns",
    )(number, *map(in_vmem, blocks))


def primal_and_members(number, minus, cost, coef):
    blocks = (CAP, BLOCK, BLOCK)
    return pl.pallas_call(
        primal_kernel,
        out_shape=(jax.ShapeDtypeStruct(blocks, jnp.bfloat16), pltpu.VMEM((MB_DEV, BLOCK), jnp.float32)),
        in_specs=[SMEM, VMEM, ANY, ANY],
        out_specs=(ANY, VMEM),
        scratch_shapes=[
            pltpu.VMEM(blocks, jnp.bfloat16),
            pltpu.VMEM(blocks, jnp.bfloat16),
            pltpu.VMEM(blocks, jnp.bfloat16),
            pltpu.VMEM((CAP, BLOCK), jnp.float32),
            pltpu.SemaphoreType.DMA((2, CHUNKS)),
            pltpu.SemaphoreType.DMA((CHUNKS,)),
        ],
        compiler_params=pltpu.CompilerParams(vmem_limit_bytes=8 * MIB),
        cost_estimate=pl.CostEstimate(
            flops=6 * CAP * BLOCK * BLOCK, bytes_accessed=6 * CAP * BLOCK * BLOCK, transcendentals=0
        ),
        name="primal",
    )(number, minus, in_hbm(cost), in_hbm(coef))


def finish(recv, share, others, capacity):
    return pl.pallas_call(
        finish_kernel,
        out_shape=(
            jax.ShapeDtypeStruct((JB_DEV, BLOCK), jnp.float32),
            jax.ShapeDtypeStruct((MB_DEV, BLOCK), jnp.float32),
        ),
        in_specs=[VMEM] * 6,
        out_specs=(VMEM, VMEM),
        compiler_params=pltpu.CompilerParams(vmem_limit_bytes=2 * 1024 * 1024),
        name="finish",
    )(recv, share, *others, capacity)


def per_device(pair_cost, pair_coef, slot_member, slot_owner, slot_local, duals, capacity):
    copies = spread(duals)
    rows = lax.all_to_all(copies, ("z", "y"), split_axis=0, concat_axis=0, tiled=True).reshape(HALF, BLOCK)
    cost, coef, named, number = stage(
        slot_owner.reshape(1, CAP), slot_local, slot_member, pair_cost, pair_coef
    )
    rows, number, late_cost, late_coef = lax.optimization_barrier((rows, number, pair_cost, pair_coef))
    other_rows = lax.ppermute(rows, "c", [(0, 1), (1, 0)])
    late_cost, late_coef = stage_late(late_cost, late_coef)
    send, minus = columns(number, named, rows, other_rows, cost, coef, late_cost, late_coef)
    send = send.reshape(MEM, 1, ROWS * BLOCK)
    recv = lax.all_to_all(send, ("z", "y", "c"), split_axis=0, concat_axis=0, tiled=True)
    primal, share = primal_and_members(number, minus, pair_cost, pair_coef)
    others = [lax.ppermute(share, "x", [(i, i ^ k) for i in range(X)]) for k in (1, 2, 3)]
    gradient, share = finish(recv, share, others, capacity)
    return primal, gradient, share


def solution(mesh):
    axes = ("z", "y", "c", "x")
    fine = Mesh(mesh.devices.reshape(Z, Y, C, X), axes)
    each = lambda n: P(axes, *([None] * (n - 1)))
    return jax.shard_map(
        per_device,
        mesh=fine,
        in_specs=(each(3), each(3), each(2), each(3), each(2), each(2), each(2)),
        out_specs=(each(3), each(2), P(("z", "y", "c"), None)),
        check_vma=False,
    )
```

```python
import jax
import jax.numpy as jnp
from jax import lax
from jax.experimental import pallas as pl
from jax.experimental.pallas import tpu as pltpu
from jax.sharding import Mesh, PartitionSpec as P

Z, Y, C, X = 8, 4, 2, 4
CAP = 48
BLOCK = 128
MB_DEV = 32
JB_DEV = 16
MEM = Z * Y * C
ROWS = 3
MIB = 1024 * 1024
EARLY = 24
LATE = CAP - EARLY
HALF = Z * Y * JB_DEV
MEMBER, ROW, OTHER, PLACE = (i * CAP for i in range(4))
VMEM = pl.BlockSpec(memory_space=pltpu.VMEM)
SMEM = pl.BlockSpec(memory_space=pltpu.SMEM)
ANY = pl.BlockSpec(memory_space=pl.ANY)


def in_hbm(a):
    return pltpu.with_memory_space_constraint(a, pltpu.HBM)


def in_vmem(a):
    return pltpu.with_memory_space_constraint(a, pltpu.VMEM)


def spread_kernel(duals_ref, out_ref, one_ref, many_ref, sem):
    load = pltpu.make_async_copy(duals_ref, one_ref, sem.at[0])
    load.start()
    load.wait()
    many_ref[...] = jnp.broadcast_to(one_ref[...][None], many_ref.shape)
    store = pltpu.make_async_copy(many_ref, out_ref, sem.at[1])
    store.start()
    store.wait()


def spread(duals):
    copies = (Z * Y, JB_DEV, BLOCK)
    return pl.pallas_call(
        spread_kernel,
        out_shape=jax.ShapeDtypeStruct(copies, jnp.float32),
        in_specs=[ANY],
        out_specs=ANY,
        scratch_shapes=[
            pltpu.VMEM((JB_DEV, BLOCK), jnp.float32),
            pltpu.VMEM(copies, jnp.float32),
            pltpu.SemaphoreType.DMA((2,)),
        ],
        compiler_params=pltpu.CompilerParams(vmem_limit_bytes=2 * MIB),
        name="spread",
    )(in_hbm(duals))


def stage_kernel(
    owner_ref, local_in_ref, member_in_ref, cost_in_ref, coef_in_ref,
    cost_ref, coef_ref, named_ref, number_ref, count_ref, sem,
):
    load_cost = pltpu.make_async_copy(cost_in_ref.at[pl.ds(0, EARLY)], cost_ref, sem.at[0])
    load_coef = pltpu.make_async_copy(coef_in_ref.at[pl.ds(0, EARLY)], coef_ref, sem.at[1])
    load_cost.start()
    load_coef.start()
    core = lax.axis_index("c")
    lane = lax.broadcasted_iota(jnp.int32, (1, BLOCK), 1)
    named_ref[...] = jnp.full((MEM, 1, BLOCK), -1.0, jnp.float32)

    def clear(i, carry):
        count_ref[i] = 0
        return carry

    lax.fori_loop(0, MEM, clear, 0)

    def slot(s, carry):
        owner = owner_ref[0, s]
        local = local_in_ref[0, s]
        number_ref[MEMBER + s] = member_in_ref[0, s]
        number_ref[ROW + s] = (owner >> 1) * JB_DEV + local
        number_ref[OTHER + s] = (owner & 1) ^ core
        k = count_ref[owner]
        count_ref[owner] = k + 1
        number_ref[PLACE + s] = owner * ROWS + k
        half = (lane >= BLOCK // 2) == (k == 1)
        named_ref[owner] = jnp.where(half, local.astype(jnp.float32), named_ref[owner])
        return carry

    lax.fori_loop(0, CAP, slot, 0)
    load_cost.wait()
    load_coef.wait()


def stage_late_kernel(cost_in_ref, coef_in_ref, cost_ref, coef_ref, sem):
    load_cost = pltpu.make_async_copy(cost_in_ref.at[pl.ds(EARLY, LATE)], cost_ref, sem.at[0])
    load_coef = pltpu.make_async_copy(coef_in_ref.at[pl.ds(EARLY, LATE)], coef_ref, sem.at[1])
    load_cost.start()
    load_coef.start()
    load_cost.wait()
    load_coef.wait()


def columns_kernel(
    number_ref, named_ref, own_rows_ref, other_rows_ref,
    early_cost_ref, early_coef_ref, late_cost_ref, late_coef_ref,
    send_ref, minus_ref, column_ref, total_ref,
):
    send_ref[...] = jnp.zeros((MEM * ROWS, 1, BLOCK), jnp.float32)
    for i in range(MEM):
        send_ref[i * ROWS + 2] = named_ref[i]
    for s in range(CAP):
        at = pl.ds(number_ref[ROW + s], 1)
        minus_ref[s:s + 1, :] = -jnp.where(number_ref[OTHER + s] == 1, other_rows_ref[at, :], own_rows_ref[at, :])

    def run(first, count, cost_ref, coef_ref):
        def block(i, carry):
            s = first + i
            minus_dual = minus_ref[pl.ds(s, 1), :]
            column = None
            for g in range(0, BLOCK, 32):
                cost = cost_ref[i, g:g + 32].astype(jnp.float32)
                coef = coef_ref[i, g:g + 32].astype(jnp.float32)
                alloc = jnp.minimum(jnp.maximum(coef * minus_dual - cost, 0.0), 1.0)
                part = jnp.sum((coef * alloc).reshape(4, 8, BLOCK), axis=0)
                column = part if column is None else column + part
            column_ref[pl.ds(pl.multiple_of(s * 8, 8), 8), :] = column
            return carry

        lax.fori_loop(0, count, block, 0, unroll=count)

    run(0, EARLY, early_cost_ref, early_coef_ref)
    run(EARLY, LATE, late_cost_ref, late_coef_ref)
    total_ref[...] = jnp.sum(column_ref[...].reshape(CAP, 8, BLOCK), axis=1)
    for s in range(CAP):
        send_ref[number_ref[PLACE + s]] = total_ref[s:s + 1, :]


def primal_kernel(
    number_ref, minus_ref, early_cost_ref, early_coef_ref, cost_in_ref, coef_in_ref,
    primal_ref, member_out_ref, late_cost_ref, late_coef_ref, sums_ref, sem,
):
    load_cost = pltpu.make_async_copy(cost_in_ref.at[pl.ds(EARLY, LATE)], late_cost_ref, sem.at[0])
    load_coef = pltpu.make_async_copy(coef_in_ref.at[pl.ds(EARLY, LATE)], late_coef_ref, sem.at[1])
    load_cost.start()
    load_coef.start()
    member_out_ref[...] = jnp.zeros((MB_DEV, BLOCK), jnp.float32)
    ones = jnp.ones((8, 2 * BLOCK), jnp.bfloat16)

    def block(s, cost_ref, coef_ref, at):
        minus_dual = minus_ref[pl.ds(s, 1), :]
        parts = []
        for g in range(0, BLOCK, 32):
            cost = cost_ref[at, g:g + 32].astype(jnp.float32)
            coef = coef_ref[at, g:g + 32].astype(jnp.float32)
            alloc = jnp.minimum(jnp.maximum(coef * minus_dual - cost, 0.0), 1.0)
            high = alloc.astype(jnp.bfloat16)
            primal_ref[s, g:g + 32] = high
            rest = (alloc - high.astype(jnp.float32)).astype(jnp.bfloat16)
            parts.append(jnp.concatenate([high, rest], axis=1))
        return parts

    def run(first, count, cost_ref, coef_ref):
        def pair(i, carry):
            s = first + 2 * i
            parts = block(s, cost_ref, coef_ref, 2 * i) + block(s + 1, cost_ref, coef_ref, 2 * i + 1)
            both = jnp.concatenate(parts, axis=0)
            sums = lax.dot_general(ones, both, (((1,), (1,)), ((), ())), preferred_element_type=jnp.float32)
            sums_ref[pl.ds(s, 1), :] = sums[0:1, :BLOCK]
            sums_ref[pl.ds(s + 1, 1), :] = sums[0:1, BLOCK:]
            return carry

        lax.fori_loop(0, count // 2, pair, 0, unroll=count // 2)

    run(0, EARLY, early_cost_ref, early_coef_ref)
    load_cost.wait()
    load_coef.wait()
    run(EARLY, LATE, late_cost_ref, late_coef_ref)
    for s in range(CAP):
        member_out_ref[pl.ds(number_ref[MEMBER + s], 1), :] += sums_ref[s:s + 1, :]


def finish_kernel(recv_ref, m0_ref, m1_ref, m2_ref, m3_ref, capacity_ref, gradient_ref, share_ref):
    share_ref[...] = ((m0_ref[...] + m1_ref[...]) + (m2_ref[...] + m3_ref[...])) * (1.0 / BLOCK)
    low = lax.broadcasted_iota(jnp.int32, (8, BLOCK), 1) < BLOCK // 2
    totals = [jnp.zeros((8, BLOCK), jnp.float32) for _ in range(JB_DEV)]
    for i in range(0, MEM, 8):
        first, second, named = (recv_ref[i:i + 8, 0, j * BLOCK:(j + 1) * BLOCK] for j in range(ROWS))
        turned = pltpu.roll(named, BLOCK // 2, 1)
        name_first = jnp.where(low, named, turned)
        name_second = jnp.where(low, turned, named)
        for k in range(JB_DEV):
            totals[k] = totals[k] + jnp.where(name_first == float(k), first, 0.0)
            totals[k] = totals[k] + jnp.where(name_second == float(k), second, 0.0)
    summed = jnp.concatenate([jnp.sum(t, axis=0, keepdims=True) for t in totals], axis=0)
    gradient_ref[...] = summed - capacity_ref[...].astype(jnp.float32)


def stage(owner, local, member, cost, coef):
    early = pltpu.VMEM((EARLY, BLOCK, BLOCK), jnp.bfloat16)
    return pl.pallas_call(
        stage_kernel,
        out_shape=(
            early,
            early,
            pltpu.VMEM((MEM, 1, BLOCK), jnp.float32),
            jax.ShapeDtypeStruct((4 * CAP,), jnp.int32),
        ),
        in_specs=[SMEM] * 3 + [ANY] * 2,
        out_specs=(VMEM, VMEM, VMEM, SMEM),
        scratch_shapes=[pltpu.SMEM((MEM,), jnp.int32), pltpu.SemaphoreType.DMA((2,))],
        compiler_params=pltpu.CompilerParams(vmem_limit_bytes=4 * 1024 * 1024),
        cost_estimate=pl.CostEstimate(flops=0, bytes_accessed=8 * EARLY * BLOCK * BLOCK, transcendentals=0),
        name="stage",
    )(owner, local, member, in_hbm(cost), in_hbm(coef))


def stage_late(cost, coef):
    late = pltpu.VMEM((LATE, BLOCK, BLOCK), jnp.bfloat16)
    return pl.pallas_call(
        stage_late_kernel,
        out_shape=(late, late),
        in_specs=[ANY] * 2,
        out_specs=(VMEM, VMEM),
        scratch_shapes=[pltpu.SemaphoreType.DMA((2,))],
        compiler_params=pltpu.CompilerParams(vmem_limit_bytes=4 * 1024 * 1024),
        cost_estimate=pl.CostEstimate(flops=0, bytes_accessed=8 * LATE * BLOCK * BLOCK, transcendentals=0),
        name="stage_late",
    )(in_hbm(cost), in_hbm(coef))


def columns(number, *blocks):
    return pl.pallas_call(
        columns_kernel,
        out_shape=(
            jax.ShapeDtypeStruct((MEM * ROWS, 1, BLOCK), jnp.float32),
            pltpu.VMEM((CAP, BLOCK), jnp.float32),
        ),
        in_specs=[SMEM] + [VMEM] * 7,
        out_specs=(VMEM, VMEM),
        scratch_shapes=[pltpu.VMEM((CAP * 8, BLOCK), jnp.float32), pltpu.VMEM((CAP, BLOCK), jnp.float32)],
        compiler_params=pltpu.CompilerParams(vmem_limit_bytes=8 * MIB),
        cost_estimate=pl.CostEstimate(
            flops=6 * CAP * BLOCK * BLOCK, bytes_accessed=4 * CAP * BLOCK * BLOCK, transcendentals=0
        ),
        name="columns",
    )(number, *map(in_vmem, blocks))


def primal_and_members(number, minus, early_cost, early_coef, cost, coef):
    late = pltpu.VMEM((LATE, BLOCK, BLOCK), jnp.bfloat16)
    return pl.pallas_call(
        primal_kernel,
        out_shape=(pltpu.VMEM((CAP, BLOCK, BLOCK), jnp.bfloat16), pltpu.VMEM((MB_DEV, BLOCK), jnp.float32)),
        in_specs=[SMEM] + [VMEM] * 3 + [ANY] * 2,
        out_specs=(VMEM, VMEM),
        scratch_shapes=[late, late, pltpu.VMEM((CAP, BLOCK), jnp.float32), pltpu.SemaphoreType.DMA((2,))],
        compiler_params=pltpu.CompilerParams(vmem_limit_bytes=8 * MIB),
        cost_estimate=pl.CostEstimate(
            flops=6 * CAP * BLOCK * BLOCK, bytes_accessed=6 * CAP * BLOCK * BLOCK, transcendentals=0
        ),
        name="primal",
    )(number, in_vmem(minus), in_vmem(early_cost), in_vmem(early_coef), in_hbm(cost), in_hbm(coef))


def finish(recv, share, others, capacity):
    return pl.pallas_call(
        finish_kernel,
        out_shape=(
            jax.ShapeDtypeStruct((JB_DEV, BLOCK), jnp.float32),
            jax.ShapeDtypeStruct((MB_DEV, BLOCK), jnp.float32),
        ),
        in_specs=[VMEM] * 6,
        out_specs=(VMEM, VMEM),
        compiler_params=pltpu.CompilerParams(vmem_limit_bytes=2 * 1024 * 1024),
        name="finish",
    )(recv, share, *others, capacity)


def per_device(pair_cost, pair_coef, slot_member, slot_owner, slot_local, duals, capacity):
    copies = spread(duals)
    rows = lax.all_to_all(copies, ("z", "y"), split_axis=0, concat_axis=0, tiled=True).reshape(HALF, BLOCK)
    cost, coef, named, number = stage(
        slot_owner.reshape(1, CAP), slot_local, slot_member, pair_cost, pair_coef
    )
    rows, number, late_cost, late_coef = lax.optimization_barrier((rows, number, pair_cost, pair_coef))
    other_rows = lax.ppermute(rows, "c", [(0, 1), (1, 0)])
    late_cost, late_coef = stage_late(late_cost, late_coef)
    send, minus = columns(number, named, rows, other_rows, cost, coef, late_cost, late_coef)
    send = send.reshape(MEM, 1, ROWS * BLOCK)
    recv = lax.all_to_all(send, ("z", "y", "c"), split_axis=0, concat_axis=0, tiled=True)
    primal, share = primal_and_members(number, minus, cost, coef, pair_cost, pair_coef)
    others = [lax.ppermute(share, "x", [(i, i ^ k) for i in range(X)]) for k in (1, 2, 3)]
    gradient, share = finish(recv, share, others, capacity)
    return primal, gradient, share


def solution(mesh):
    axes = ("z", "y", "c", "x")
    fine = Mesh(mesh.devices.reshape(Z, Y, C, X), axes)
    each = lambda n: P(axes, *([None] * (n - 1)))
    return jax.shard_map(
        per_device,
        mesh=fine,
        in_specs=(each(3), each(3), each(2), each(3), each(2), each(2), each(2)),
        out_specs=(each(3), each(2), P(("z", "y", "c"), None)),
        check_vma=False,
    )
```

```python
import jax
import jax.numpy as jnp
from jax import lax
from jax.experimental import pallas as pl
from jax.experimental.pallas import tpu as pltpu
from jax.sharding import Mesh, PartitionSpec as P

Z, Y, C, X = 8, 4, 2, 4
CAP = 48
BLOCK = 128
MB_DEV = 32
JB_DEV = 16
MEM = Z * Y * C
ROWS = 3
MIB = 1024 * 1024
EARLY = 24
LATE = CAP - EARLY
HALF = Z * Y * JB_DEV
MEMBER, ROW, OTHER, PLACE = (i * CAP for i in range(4))
VMEM = pl.BlockSpec(memory_space=pltpu.VMEM)
SMEM = pl.BlockSpec(memory_space=pltpu.SMEM)
ANY = pl.BlockSpec(memory_space=pl.ANY)


def in_hbm(a):
    return pltpu.with_memory_space_constraint(a, pltpu.HBM)


def in_vmem(a):
    return pltpu.with_memory_space_constraint(a, pltpu.VMEM)


def spread_kernel(duals_ref, out_ref, one_ref, many_ref, sem):
    load = pltpu.make_async_copy(duals_ref, one_ref, sem.at[0])
    load.start()
    load.wait()
    many_ref[...] = jnp.broadcast_to(one_ref[...][None], many_ref.shape)
    store = pltpu.make_async_copy(many_ref, out_ref, sem.at[1])
    store.start()
    store.wait()


def spread(duals):
    copies = (Z * Y, JB_DEV, BLOCK)
    return pl.pallas_call(
        spread_kernel,
        out_shape=jax.ShapeDtypeStruct(copies, jnp.float32),
        in_specs=[ANY],
        out_specs=ANY,
        scratch_shapes=[
            pltpu.VMEM((JB_DEV, BLOCK), jnp.float32),
            pltpu.VMEM(copies, jnp.float32),
            pltpu.SemaphoreType.DMA((2,)),
        ],
        compiler_params=pltpu.CompilerParams(vmem_limit_bytes=2 * MIB),
        name="spread",
    )(in_hbm(duals))


def stage_kernel(
    owner_ref, local_in_ref, member_in_ref, coef_in_ref,
    early_ref, late_ref, named_ref, number_ref, count_ref, sem,
):
    load_early = pltpu.make_async_copy(coef_in_ref.at[pl.ds(0, EARLY)], early_ref, sem.at[0])
    load_late = pltpu.make_async_copy(coef_in_ref.at[pl.ds(EARLY, LATE)], late_ref, sem.at[1])
    load_early.start()
    load_late.start()
    core = lax.axis_index("c")
    lane = lax.broadcasted_iota(jnp.int32, (1, BLOCK), 1)
    named_ref[...] = jnp.full((MEM, 1, BLOCK), -1.0, jnp.float32)

    def clear(i, carry):
        count_ref[i] = 0
        return carry

    lax.fori_loop(0, MEM, clear, 0)

    def slot(s, carry):
        owner = owner_ref[0, s]
        local = local_in_ref[0, s]
        number_ref[MEMBER + s] = member_in_ref[0, s]
        number_ref[ROW + s] = (owner >> 1) * JB_DEV + local
        number_ref[OTHER + s] = (owner & 1) ^ core
        k = count_ref[owner]
        count_ref[owner] = k + 1
        number_ref[PLACE + s] = owner * ROWS + k
        half = (lane >= BLOCK // 2) == (k == 1)
        named_ref[owner] = jnp.where(half, local.astype(jnp.float32), named_ref[owner])
        return carry

    lax.fori_loop(0, CAP, slot, 0)
    load_early.wait()
    load_late.wait()


def columns_kernel(
    number_ref, named_ref, own_rows_ref, other_rows_ref,
    cost_ref, early_coef_ref, late_coef_ref,
    send_ref, minus_ref, column_ref, total_ref,
):
    send_ref[...] = jnp.zeros((MEM * ROWS, 1, BLOCK), jnp.float32)
    for i in range(MEM):
        send_ref[i * ROWS + 2] = named_ref[i]
    for s in range(CAP):
        at = pl.ds(number_ref[ROW + s], 1)
        minus_ref[s:s + 1, :] = -jnp.where(number_ref[OTHER + s] == 1, other_rows_ref[at, :], own_rows_ref[at, :])

    def run(first, count, coef_ref):
        def block(i, carry):
            s = first + i
            minus_dual = minus_ref[pl.ds(s, 1), :]
            column = None
            for g in range(0, BLOCK, 32):
                cost = cost_ref[s, g:g + 32].astype(jnp.float32)
                coef = coef_ref[i, g:g + 32].astype(jnp.float32)
                alloc = jnp.minimum(jnp.maximum(coef * minus_dual - cost, 0.0), 1.0)
                part = jnp.sum((coef * alloc).reshape(4, 8, BLOCK), axis=0)
                column = part if column is None else column + part
            column_ref[pl.ds(pl.multiple_of(s * 8, 8), 8), :] = column
            return carry

        lax.fori_loop(0, count, block, 0, unroll=count)

    run(0, EARLY, early_coef_ref)
    run(EARLY, LATE, late_coef_ref)
    total_ref[...] = jnp.sum(column_ref[...].reshape(CAP, 8, BLOCK), axis=1)
    for s in range(CAP):
        send_ref[number_ref[PLACE + s]] = total_ref[s:s + 1, :]


def primal_kernel(
    number_ref, minus_ref, early_coef_ref, late_coef_ref, cost_in_ref,
    primal_ref, member_out_ref, early_cost_ref, late_cost_ref, sums_ref, sem,
):
    load_early = pltpu.make_async_copy(cost_in_ref.at[pl.ds(0, EARLY)], early_cost_ref, sem.at[0])
    load_late = pltpu.make_async_copy(cost_in_ref.at[pl.ds(EARLY, LATE)], late_cost_ref, sem.at[1])
    load_early.start()
    load_late.start()
    member_out_ref[...] = jnp.zeros((MB_DEV, BLOCK), jnp.float32)
    ones = jnp.ones((8, 2 * BLOCK), jnp.bfloat16)

    def block(s, cost_ref, coef_ref, at):
        minus_dual = minus_ref[pl.ds(s, 1), :]
        parts = []
        for g in range(0, BLOCK, 32):
            cost = cost_ref[at, g:g + 32].astype(jnp.float32)
            coef = coef_ref[at, g:g + 32].astype(jnp.float32)
            alloc = jnp.minimum(jnp.maximum(coef * minus_dual - cost, 0.0), 1.0)
            high = alloc.astype(jnp.bfloat16)
            primal_ref[s, g:g + 32] = high
            rest = (alloc - high.astype(jnp.float32)).astype(jnp.bfloat16)
            parts.append(jnp.concatenate([high, rest], axis=1))
        return parts

    def run(first, count, cost_ref, coef_ref):
        def pair(i, carry):
            s = first + 2 * i
            parts = block(s, cost_ref, coef_ref, 2 * i) + block(s + 1, cost_ref, coef_ref, 2 * i + 1)
            both = jnp.concatenate(parts, axis=0)
            sums = lax.dot_general(ones, both, (((1,), (1,)), ((), ())), preferred_element_type=jnp.float32)
            sums_ref[pl.ds(s, 1), :] = sums[0:1, :BLOCK]
            sums_ref[pl.ds(s + 1, 1), :] = sums[0:1, BLOCK:]
            return carry

        lax.fori_loop(0, count // 2, pair, 0, unroll=count // 2)

    load_early.wait()
    run(0, EARLY, early_cost_ref, early_coef_ref)
    load_late.wait()
    run(EARLY, LATE, late_cost_ref, late_coef_ref)
    for s in range(CAP):
        member_out_ref[pl.ds(number_ref[MEMBER + s], 1), :] += sums_ref[s:s + 1, :]


def finish_kernel(recv_ref, m0_ref, m1_ref, m2_ref, m3_ref, capacity_ref, gradient_ref, share_ref):
    share_ref[...] = ((m0_ref[...] + m1_ref[...]) + (m2_ref[...] + m3_ref[...])) * (1.0 / BLOCK)
    low = lax.broadcasted_iota(jnp.int32, (8, BLOCK), 1) < BLOCK // 2
    totals = [jnp.zeros((8, BLOCK), jnp.float32) for _ in range(JB_DEV)]
    for i in range(0, MEM, 8):
        first, second, named = (recv_ref[i:i + 8, 0, j * BLOCK:(j + 1) * BLOCK] for j in range(ROWS))
        turned = pltpu.roll(named, BLOCK // 2, 1)
        name_first = jnp.where(low, named, turned)
        name_second = jnp.where(low, turned, named)
        for k in range(JB_DEV):
            totals[k] = totals[k] + jnp.where(name_first == float(k), first, 0.0)
            totals[k] = totals[k] + jnp.where(name_second == float(k), second, 0.0)
    summed = jnp.concatenate([jnp.sum(t, axis=0, keepdims=True) for t in totals], axis=0)
    gradient_ref[...] = summed - capacity_ref[...].astype(jnp.float32)


def stage(owner, local, member, coef):
    early = pltpu.VMEM((EARLY, BLOCK, BLOCK), jnp.bfloat16)
    return pl.pallas_call(
        stage_kernel,
        out_shape=(
            early,
            early,
            pltpu.VMEM((MEM, 1, BLOCK), jnp.float32),
            jax.ShapeDtypeStruct((4 * CAP,), jnp.int32),
        ),
        in_specs=[SMEM] * 3 + [ANY],
        out_specs=(VMEM, VMEM, VMEM, SMEM),
        scratch_shapes=[pltpu.SMEM((MEM,), jnp.int32), pltpu.SemaphoreType.DMA((2,))],
        compiler_params=pltpu.CompilerParams(vmem_limit_bytes=4 * 1024 * 1024),
        cost_estimate=pl.CostEstimate(flops=0, bytes_accessed=8 * EARLY * BLOCK * BLOCK, transcendentals=0),
        name="stage",
    )(owner, local, member, in_hbm(coef))


def columns(number, *blocks):
    return pl.pallas_call(
        columns_kernel,
        out_shape=(
            jax.ShapeDtypeStruct((MEM * ROWS, 1, BLOCK), jnp.float32),
            pltpu.VMEM((CAP, BLOCK), jnp.float32),
        ),
        in_specs=[SMEM] + [VMEM] * 6,
        out_specs=(VMEM, VMEM),
        scratch_shapes=[pltpu.VMEM((CAP * 8, BLOCK), jnp.float32), pltpu.VMEM((CAP, BLOCK), jnp.float32)],
        compiler_params=pltpu.CompilerParams(vmem_limit_bytes=8 * MIB),
        cost_estimate=pl.CostEstimate(
            flops=6 * CAP * BLOCK * BLOCK, bytes_accessed=4 * CAP * BLOCK * BLOCK, transcendentals=0
        ),
        name="columns",
    )(number, *map(in_vmem, blocks))


def primal_and_members(number, minus, early_coef, late_coef, cost):
    half = pltpu.VMEM((EARLY, BLOCK, BLOCK), jnp.bfloat16)
    return pl.pallas_call(
        primal_kernel,
        out_shape=(pltpu.VMEM((CAP, BLOCK, BLOCK), jnp.bfloat16), pltpu.VMEM((MB_DEV, BLOCK), jnp.float32)),
        in_specs=[SMEM] + [VMEM] * 3 + [ANY],
        out_specs=(VMEM, VMEM),
        scratch_shapes=[half, half, pltpu.VMEM((CAP, BLOCK), jnp.float32), pltpu.SemaphoreType.DMA((2,))],
        compiler_params=pltpu.CompilerParams(vmem_limit_bytes=8 * MIB),
        cost_estimate=pl.CostEstimate(
            flops=6 * CAP * BLOCK * BLOCK, bytes_accessed=6 * CAP * BLOCK * BLOCK, transcendentals=0
        ),
        name="primal",
    )(number, in_vmem(minus), in_vmem(early_coef), in_vmem(late_coef), in_hbm(cost))


def finish(recv, share, others, capacity):
    return pl.pallas_call(
        finish_kernel,
        out_shape=(
            jax.ShapeDtypeStruct((JB_DEV, BLOCK), jnp.float32),
            jax.ShapeDtypeStruct((MB_DEV, BLOCK), jnp.float32),
        ),
        in_specs=[VMEM] * 6,
        out_specs=(VMEM, VMEM),
        compiler_params=pltpu.CompilerParams(vmem_limit_bytes=2 * 1024 * 1024),
        name="finish",
    )(recv, share, *others, capacity)


def per_device(pair_cost, pair_coef, slot_member, slot_owner, slot_local, duals, capacity):
    copies = spread(duals)
    rows = lax.all_to_all(copies, ("z", "y"), split_axis=0, concat_axis=0, tiled=True).reshape(HALF, BLOCK)
    early, late, named, number = stage(slot_owner.reshape(1, CAP), slot_local, slot_member, pair_coef)
    rows, number = lax.optimization_barrier((rows, number))
    other_rows = lax.ppermute(rows, "c", [(0, 1), (1, 0)])
    send, minus = columns(number, named, rows, other_rows, pair_cost, early, late)
    send = send.reshape(MEM, 1, ROWS * BLOCK)
    recv = lax.all_to_all(send, ("z", "y", "c"), split_axis=0, concat_axis=0, tiled=True)
    primal, share = primal_and_members(number, minus, early, late, pair_cost)
    others = [lax.ppermute(share, "x", [(i, i ^ k) for i in range(X)]) for k in (1, 2, 3)]
    gradient, share = finish(recv, share, others, capacity)
    return primal, gradient, share


def solution(mesh):
    axes = ("z", "y", "c", "x")
    fine = Mesh(mesh.devices.reshape(Z, Y, C, X), axes)
    each = lambda n: P(axes, *([None] * (n - 1)))
    return jax.shard_map(
        per_device,
        mesh=fine,
        in_specs=(each(3), each(3), each(2), each(3), each(2), each(2), each(2)),
        out_specs=(each(3), each(2), P(("z", "y", "c"), None)),
        check_vma=False,
    )
```

```python
import jax
import jax.numpy as jnp
from jax import lax
from jax.experimental import pallas as pl
from jax.experimental.pallas import tpu as pltpu
from jax.sharding import Mesh, PartitionSpec as P

Z, Y, C, X = 8, 4, 2, 4
CAP = 48
BLOCK = 128
MB_DEV = 32
JB_DEV = 16
MEM = Z * Y * C
ROWS = 3
MIB = 1024 * 1024
EARLY = 24
LATE = CAP - EARLY
HALF = Z * Y * JB_DEV
MEMBER, ROW, OTHER, PLACE = (i * CAP for i in range(4))
VMEM = pl.BlockSpec(memory_space=pltpu.VMEM)
SMEM = pl.BlockSpec(memory_space=pltpu.SMEM)
ANY = pl.BlockSpec(memory_space=pl.ANY)


def in_hbm(a):
    return pltpu.with_memory_space_constraint(a, pltpu.HBM)


def in_vmem(a):
    return pltpu.with_memory_space_constraint(a, pltpu.VMEM)


def spread_kernel(duals_ref, out_ref, one_ref, many_ref, sem):
    load = pltpu.make_async_copy(duals_ref, one_ref, sem.at[0])
    load.start()
    load.wait()
    many_ref[...] = jnp.broadcast_to(one_ref[...][None], many_ref.shape)
    store = pltpu.make_async_copy(many_ref, out_ref, sem.at[1])
    store.start()
    store.wait()


def spread(duals):
    copies = (Z * Y, JB_DEV, BLOCK)
    return pl.pallas_call(
        spread_kernel,
        out_shape=jax.ShapeDtypeStruct(copies, jnp.float32),
        in_specs=[ANY],
        out_specs=ANY,
        scratch_shapes=[
            pltpu.VMEM((JB_DEV, BLOCK), jnp.float32),
            pltpu.VMEM(copies, jnp.float32),
            pltpu.SemaphoreType.DMA((2,)),
        ],
        compiler_params=pltpu.CompilerParams(vmem_limit_bytes=2 * MIB),
        name="spread",
    )(in_hbm(duals))


def stage_kernel(
    owner_ref, local_in_ref, member_in_ref, cost_in_ref, coef_in_ref,
    cost_ref, coef_ref, named_ref, number_ref, count_ref, sem,
):
    load_cost = pltpu.make_async_copy(cost_in_ref.at[pl.ds(0, EARLY)], cost_ref, sem.at[0])
    load_coef = pltpu.make_async_copy(coef_in_ref.at[pl.ds(0, EARLY)], coef_ref, sem.at[1])
    load_cost.start()
    load_coef.start()
    core = lax.axis_index("c")
    lane = lax.broadcasted_iota(jnp.int32, (1, BLOCK), 1)
    named_ref[...] = jnp.zeros((MEM * ROWS, 1, BLOCK), jnp.float32)
    for i in range(MEM):
        named_ref[i * ROWS + 2] = jnp.full((1, BLOCK), -1.0, jnp.float32)

    def clear(i, carry):
        count_ref[i] = 0
        return carry

    lax.fori_loop(0, MEM, clear, 0)

    def slot(s, carry):
        owner = owner_ref[0, s]
        local = local_in_ref[0, s]
        number_ref[MEMBER + s] = member_in_ref[0, s]
        number_ref[ROW + s] = (owner >> 1) * JB_DEV + local
        number_ref[OTHER + s] = (owner & 1) ^ core
        k = count_ref[owner]
        count_ref[owner] = k + 1
        number_ref[PLACE + s] = owner * ROWS + k
        half = (lane >= BLOCK // 2) == (k == 1)
        at = owner * ROWS + 2
        named_ref[at] = jnp.where(half, local.astype(jnp.float32), named_ref[at])
        return carry

    lax.fori_loop(0, CAP, slot, 0)
    load_cost.wait()
    load_coef.wait()


def stage_late_kernel(cost_in_ref, coef_in_ref, cost_ref, coef_ref, sem):
    load_cost = pltpu.make_async_copy(cost_in_ref.at[pl.ds(EARLY, LATE)], cost_ref, sem.at[0])
    load_coef = pltpu.make_async_copy(coef_in_ref.at[pl.ds(EARLY, LATE)], coef_ref, sem.at[1])
    load_cost.start()
    load_coef.start()
    load_cost.wait()
    load_coef.wait()


def columns_kernel(
    number_ref, named_ref, own_rows_ref, other_rows_ref,
    early_cost_ref, early_coef_ref, late_cost_ref, late_coef_ref,
    send_ref, minus_ref, column_ref, total_ref,
):
    send_ref[...] = named_ref[...]
    for s in range(CAP):
        at = pl.ds(number_ref[ROW + s], 1)
        minus_ref[s:s + 1, :] = -jnp.where(number_ref[OTHER + s] == 1, other_rows_ref[at, :], own_rows_ref[at, :])

    def run(first, count, cost_ref, coef_ref):
        def block(i, carry):
            s = first + i
            minus_dual = minus_ref[pl.ds(s, 1), :]
            column = None
            for g in range(0, BLOCK, 32):
                cost = cost_ref[i, g:g + 32].astype(jnp.float32)
                coef = coef_ref[i, g:g + 32].astype(jnp.float32)
                alloc = jnp.minimum(jnp.maximum(coef * minus_dual - cost, 0.0), 1.0)
                part = jnp.sum((coef * alloc).reshape(4, 8, BLOCK), axis=0)
                column = part if column is None else column + part
            column_ref[pl.ds(pl.multiple_of(s * 8, 8), 8), :] = column
            return carry

        lax.fori_loop(0, count, block, 0, unroll=count)

    run(0, EARLY, early_cost_ref, early_coef_ref)
    run(EARLY, LATE, late_cost_ref, late_coef_ref)
    total_ref[...] = jnp.sum(column_ref[...].reshape(CAP, 8, BLOCK), axis=1)
    for s in range(CAP):
        send_ref[number_ref[PLACE + s]] = total_ref[s:s + 1, :]


def primal_kernel(
    number_ref, minus_ref, early_cost_ref, early_coef_ref, cost_in_ref, coef_in_ref,
    primal_ref, member_out_ref, late_cost_ref, late_coef_ref, sums_ref, sem,
):
    load_cost = pltpu.make_async_copy(cost_in_ref.at[pl.ds(EARLY, LATE)], late_cost_ref, sem.at[0])
    load_coef = pltpu.make_async_copy(coef_in_ref.at[pl.ds(EARLY, LATE)], late_coef_ref, sem.at[1])
    load_cost.start()
    load_coef.start()
    member_out_ref[...] = jnp.zeros((MB_DEV, BLOCK), jnp.float32)
    ones = jnp.ones((8, 2 * BLOCK), jnp.bfloat16)

    def block(s, cost_ref, coef_ref, at):
        minus_dual = minus_ref[pl.ds(s, 1), :]
        parts = []
        for g in range(0, BLOCK, 32):
            cost = cost_ref[at, g:g + 32].astype(jnp.float32)
            coef = coef_ref[at, g:g + 32].astype(jnp.float32)
            alloc = jnp.minimum(jnp.maximum(coef * minus_dual - cost, 0.0), 1.0)
            high = alloc.astype(jnp.bfloat16)
            primal_ref[s, g:g + 32] = high
            rest = (alloc - high.astype(jnp.float32)).astype(jnp.bfloat16)
            parts.append(jnp.concatenate([high, rest], axis=1))
        return parts

    def run(first, count, cost_ref, coef_ref):
        def pair(i, carry):
            s = first + 2 * i
            parts = block(s, cost_ref, coef_ref, 2 * i) + block(s + 1, cost_ref, coef_ref, 2 * i + 1)
            both = jnp.concatenate(parts, axis=0)
            sums = lax.dot_general(ones, both, (((1,), (1,)), ((), ())), preferred_element_type=jnp.float32)
            sums_ref[pl.ds(s, 1), :] = sums[0:1, :BLOCK]
            sums_ref[pl.ds(s + 1, 1), :] = sums[0:1, BLOCK:]
            return carry

        lax.fori_loop(0, count // 2, pair, 0, unroll=count // 2)

    run(0, EARLY, early_cost_ref, early_coef_ref)
    load_cost.wait()
    load_coef.wait()
    run(EARLY, LATE, late_cost_ref, late_coef_ref)
    for s in range(CAP):
        member_out_ref[pl.ds(number_ref[MEMBER + s], 1), :] += sums_ref[s:s + 1, :]


def finish_kernel(recv_ref, capacity_ref, gradient_ref):
    low = lax.broadcasted_iota(jnp.int32, (8, BLOCK), 1) < BLOCK // 2
    totals = [jnp.zeros((8, BLOCK), jnp.float32) for _ in range(JB_DEV)]
    for i in range(0, MEM, 8):
        first, second, named = (recv_ref[i:i + 8, 0, j * BLOCK:(j + 1) * BLOCK] for j in range(ROWS))
        turned = pltpu.roll(named, BLOCK // 2, 1)
        name_first = jnp.where(low, named, turned)
        name_second = jnp.where(low, turned, named)
        for k in range(JB_DEV):
            totals[k] = totals[k] + jnp.where(name_first == float(k), first, 0.0)
            totals[k] = totals[k] + jnp.where(name_second == float(k), second, 0.0)
    summed = jnp.concatenate([jnp.sum(t, axis=0, keepdims=True) for t in totals], axis=0)
    gradient_ref[...] = summed - capacity_ref[...].astype(jnp.float32)


def stage(owner, local, member, cost, coef):
    early = pltpu.VMEM((EARLY, BLOCK, BLOCK), jnp.bfloat16)
    return pl.pallas_call(
        stage_kernel,
        out_shape=(
            early,
            early,
            pltpu.VMEM((MEM * ROWS, 1, BLOCK), jnp.float32),
            jax.ShapeDtypeStruct((4 * CAP,), jnp.int32),
        ),
        in_specs=[SMEM] * 3 + [ANY] * 2,
        out_specs=(VMEM, VMEM, VMEM, SMEM),
        scratch_shapes=[pltpu.SMEM((MEM,), jnp.int32), pltpu.SemaphoreType.DMA((2,))],
        compiler_params=pltpu.CompilerParams(vmem_limit_bytes=4 * 1024 * 1024),
        cost_estimate=pl.CostEstimate(flops=0, bytes_accessed=8 * EARLY * BLOCK * BLOCK, transcendentals=0),
        name="stage",
    )(owner, local, member, in_hbm(cost), in_hbm(coef))


def stage_late(cost, coef):
    late = pltpu.VMEM((LATE, BLOCK, BLOCK), jnp.bfloat16)
    return pl.pallas_call(
        stage_late_kernel,
        out_shape=(late, late),
        in_specs=[ANY] * 2,
        out_specs=(VMEM, VMEM),
        scratch_shapes=[pltpu.SemaphoreType.DMA((2,))],
        compiler_params=pltpu.CompilerParams(vmem_limit_bytes=4 * 1024 * 1024),
        cost_estimate=pl.CostEstimate(flops=0, bytes_accessed=8 * LATE * BLOCK * BLOCK, transcendentals=0),
        name="stage_late",
    )(in_hbm(cost), in_hbm(coef))


def columns(number, *blocks):
    return pl.pallas_call(
        columns_kernel,
        out_shape=(
            jax.ShapeDtypeStruct((MEM * ROWS, 1, BLOCK), jnp.float32),
            pltpu.VMEM((CAP, BLOCK), jnp.float32),
        ),
        in_specs=[SMEM] + [VMEM] * 7,
        out_specs=(VMEM, VMEM),
        scratch_shapes=[pltpu.VMEM((CAP * 8, BLOCK), jnp.float32), pltpu.VMEM((CAP, BLOCK), jnp.float32)],
        compiler_params=pltpu.CompilerParams(vmem_limit_bytes=8 * MIB),
        cost_estimate=pl.CostEstimate(
            flops=6 * CAP * BLOCK * BLOCK, bytes_accessed=4 * CAP * BLOCK * BLOCK, transcendentals=0
        ),
        name="columns",
    )(number, *map(in_vmem, blocks))


def primal_and_members(number, minus, early_cost, early_coef, cost, coef):
    late = pltpu.VMEM((LATE, BLOCK, BLOCK), jnp.bfloat16)
    return pl.pallas_call(
        primal_kernel,
        out_shape=(pltpu.VMEM((CAP, BLOCK, BLOCK), jnp.bfloat16), pltpu.VMEM((MB_DEV, BLOCK), jnp.float32)),
        in_specs=[SMEM] + [VMEM] * 3 + [ANY] * 2,
        out_specs=(VMEM, VMEM),
        scratch_shapes=[late, late, pltpu.VMEM((CAP, BLOCK), jnp.float32), pltpu.SemaphoreType.DMA((2,))],
        compiler_params=pltpu.CompilerParams(vmem_limit_bytes=8 * MIB),
        cost_estimate=pl.CostEstimate(
            flops=6 * CAP * BLOCK * BLOCK, bytes_accessed=6 * CAP * BLOCK * BLOCK, transcendentals=0
        ),
        name="primal",
    )(number, in_vmem(minus), in_vmem(early_cost), in_vmem(early_coef), in_hbm(cost), in_hbm(coef))


def finish(recv, capacity):
    return pl.pallas_call(
        finish_kernel,
        out_shape=jax.ShapeDtypeStruct((JB_DEV, BLOCK), jnp.float32),
        in_specs=[VMEM] * 2,
        out_specs=VMEM,
        compiler_params=pltpu.CompilerParams(vmem_limit_bytes=2 * MIB),
        name="finish",
    )(recv, capacity)


def per_device(pair_cost, pair_coef, slot_member, slot_owner, slot_local, duals, capacity):
    copies = spread(duals)
    rows = lax.all_to_all(copies, ("z", "y"), split_axis=0, concat_axis=0, tiled=True).reshape(HALF, BLOCK)
    cost, coef, named, number = stage(
        slot_owner.reshape(1, CAP), slot_local, slot_member, pair_cost, pair_coef
    )
    rows, number, late_cost, late_coef = lax.optimization_barrier((rows, number, pair_cost, pair_coef))
    other_rows = lax.ppermute(rows, "c", [(0, 1), (1, 0)])
    late_cost, late_coef = stage_late(late_cost, late_coef)
    send, minus = columns(number, named, rows, other_rows, cost, coef, late_cost, late_coef)
    send = send.reshape(MEM, 1, ROWS * BLOCK)
    recv = lax.all_to_all(send, ("z", "y", "c"), split_axis=0, concat_axis=0, tiled=True)
    primal, share = primal_and_members(number, minus, cost, coef, pair_cost, pair_coef)
    others = [lax.ppermute(share, "x", [(i, i ^ k) for i in range(X)]) for k in (1, 2, 3)]
    share = ((share + others[0]) + (others[1] + others[2])) * (1.0 / BLOCK)
    gradient = finish(recv, capacity)
    return primal, gradient, share


def solution(mesh):
    axes = ("z", "y", "c", "x")
    fine = Mesh(mesh.devices.reshape(Z, Y, C, X), axes)
    each = lambda n: P(axes, *([None] * (n - 1)))
    return jax.shard_map(
        per_device,
        mesh=fine,
        in_specs=(each(3), each(3), each(2), each(3), each(2), each(2), each(2)),
        out_specs=(each(3), each(2), P(("z", "y", "c"), None)),
        check_vma=False,
    )
```

```python
import jax
import jax.numpy as jnp
from jax import lax
from jax.experimental import pallas as pl
from jax.experimental.pallas import tpu as pltpu
from jax.sharding import Mesh, PartitionSpec as P

Z, Y, C, X = 8, 4, 2, 4
CAP = 48
BLOCK = 128
MB_DEV = 32
JB_DEV = 16
MEM = Z * Y * C
ROWS = 3
MIB = 1024 * 1024
EARLY = 24
LATE = CAP - EARLY
HALF = Z * Y * JB_DEV
MEMBER, ROW, OTHER, PLACE = (i * CAP for i in range(4))
VMEM = pl.BlockSpec(memory_space=pltpu.VMEM)
SMEM = pl.BlockSpec(memory_space=pltpu.SMEM)
ANY = pl.BlockSpec(memory_space=pl.ANY)


def in_hbm(a):
    return pltpu.with_memory_space_constraint(a, pltpu.HBM)


def in_vmem(a):
    return pltpu.with_memory_space_constraint(a, pltpu.VMEM)


def spread_kernel(duals_ref, out_ref, one_ref, many_ref, sem):
    load = pltpu.make_async_copy(duals_ref, one_ref, sem.at[0])
    load.start()
    load.wait()
    many_ref[...] = jnp.broadcast_to(one_ref[...][None], many_ref.shape)
    store = pltpu.make_async_copy(many_ref, out_ref, sem.at[1])
    store.start()
    store.wait()


def spread(duals):
    copies = (Z * Y, JB_DEV, BLOCK)
    return pl.pallas_call(
        spread_kernel,
        out_shape=jax.ShapeDtypeStruct(copies, jnp.float32),
        in_specs=[ANY],
        out_specs=ANY,
        scratch_shapes=[
            pltpu.VMEM((JB_DEV, BLOCK), jnp.float32),
            pltpu.VMEM(copies, jnp.float32),
            pltpu.SemaphoreType.DMA((2,)),
        ],
        compiler_params=pltpu.CompilerParams(vmem_limit_bytes=2 * MIB),
        name="spread",
    )(in_hbm(duals))


def stage_kernel(
    owner_ref, local_in_ref, member_in_ref, cost_in_ref, coef_in_ref,
    cost_ref, coef_ref, named_ref, number_ref, count_ref, sem,
):
    load_cost = pltpu.make_async_copy(cost_in_ref.at[pl.ds(0, EARLY)], cost_ref, sem.at[0])
    load_coef = pltpu.make_async_copy(coef_in_ref.at[pl.ds(0, EARLY)], coef_ref, sem.at[1])
    load_cost.start()
    load_coef.start()
    core = lax.axis_index("c")
    lane = lax.broadcasted_iota(jnp.int32, (1, BLOCK), 1)
    named_ref[...] = jnp.zeros((MEM * ROWS, 1, BLOCK), jnp.float32)
    for i in range(MEM):
        named_ref[i * ROWS + 2] = jnp.full((1, BLOCK), -1.0, jnp.float32)

    def clear(i, carry):
        count_ref[i] = 0
        return carry

    lax.fori_loop(0, MEM, clear, 0)

    def slot(s, carry):
        owner = owner_ref[0, s]
        local = local_in_ref[0, s]
        number_ref[MEMBER + s] = member_in_ref[0, s]
        number_ref[ROW + s] = (owner >> 1) * JB_DEV + local
        number_ref[OTHER + s] = (owner & 1) ^ core
        k = count_ref[owner]
        count_ref[owner] = k + 1
        number_ref[PLACE + s] = owner * ROWS + k
        half = (lane >= BLOCK // 2) == (k == 1)
        at = owner * ROWS + 2
        named_ref[at] = jnp.where(half, local.astype(jnp.float32), named_ref[at])
        return carry

    lax.fori_loop(0, CAP, slot, 0)
    load_cost.wait()
    load_coef.wait()


def stage_late_kernel(cost_in_ref, coef_in_ref, cost_ref, coef_ref, sem):
    load_cost = pltpu.make_async_copy(cost_in_ref.at[pl.ds(EARLY, LATE)], cost_ref, sem.at[0])
    load_coef = pltpu.make_async_copy(coef_in_ref.at[pl.ds(EARLY, LATE)], coef_ref, sem.at[1])
    load_cost.start()
    load_coef.start()
    load_cost.wait()
    load_coef.wait()


def columns_kernel(
    number_ref, named_ref, own_rows_ref, other_rows_ref,
    early_cost_ref, early_coef_ref, late_cost_ref, late_coef_ref,
    send_ref, minus_ref, column_ref, total_ref,
):
    send_ref[...] = named_ref[...]
    for s in range(CAP):
        at = pl.ds(number_ref[ROW + s], 1)
        minus_ref[s:s + 1, :] = -jnp.where(number_ref[OTHER + s] == 1, other_rows_ref[at, :], own_rows_ref[at, :])

    def run(first, count, cost_ref, coef_ref):
        def block(i, carry):
            s = first + i
            minus_dual = minus_ref[pl.ds(s, 1), :]
            column = None
            for g in range(0, BLOCK, 32):
                cost = cost_ref[i, g:g + 32].astype(jnp.float32)
                coef = coef_ref[i, g:g + 32].astype(jnp.float32)
                alloc = jnp.minimum(jnp.maximum(coef * minus_dual - cost, 0.0), 1.0)
                part = jnp.sum((coef * alloc).reshape(4, 8, BLOCK), axis=0)
                column = part if column is None else column + part
            column_ref[pl.ds(pl.multiple_of(s * 8, 8), 8), :] = column
            return carry

        lax.fori_loop(0, count, block, 0, unroll=count)

    run(0, EARLY, early_cost_ref, early_coef_ref)
    run(EARLY, LATE, late_cost_ref, late_coef_ref)
    total_ref[...] = jnp.sum(column_ref[...].reshape(CAP, 8, BLOCK), axis=1)
    for s in range(CAP):
        send_ref[number_ref[PLACE + s]] = total_ref[s:s + 1, :]


def primal_kernel(
    number_ref, minus_ref, early_cost_ref, early_coef_ref, cost_in_ref, coef_in_ref,
    primal_ref, member_out_ref, late_cost_ref, late_coef_ref, sums_ref, sem,
):
    load_cost = pltpu.make_async_copy(cost_in_ref.at[pl.ds(EARLY, LATE)], late_cost_ref, sem.at[0])
    load_coef = pltpu.make_async_copy(coef_in_ref.at[pl.ds(EARLY, LATE)], late_coef_ref, sem.at[1])
    load_cost.start()
    load_coef.start()
    member_out_ref[...] = jnp.zeros((MB_DEV, BLOCK), jnp.float32)
    ones = jnp.ones((8, 2 * BLOCK), jnp.bfloat16)

    def block(s, cost_ref, coef_ref, at):
        minus_dual = minus_ref[pl.ds(s, 1), :]
        parts = []
        for g in range(0, BLOCK, 32):
            cost = cost_ref[at, g:g + 32].astype(jnp.float32)
            coef = coef_ref[at, g:g + 32].astype(jnp.float32)
            alloc = jnp.minimum(jnp.maximum(coef * minus_dual - cost, 0.0), 1.0)
            high = alloc.astype(jnp.bfloat16)
            primal_ref[s, g:g + 32] = high
            rest = (alloc - high.astype(jnp.float32)).astype(jnp.bfloat16)
            parts.append(jnp.concatenate([high, rest], axis=1))
        return parts

    def run(first, count, cost_ref, coef_ref):
        def pair(i, carry):
            s = first + 2 * i
            parts = block(s, cost_ref, coef_ref, 2 * i) + block(s + 1, cost_ref, coef_ref, 2 * i + 1)
            both = jnp.concatenate(parts, axis=0)
            sums = lax.dot_general(ones, both, (((1,), (1,)), ((), ())), preferred_element_type=jnp.float32)
            sums_ref[pl.ds(s, 1), :] = sums[0:1, :BLOCK]
            sums_ref[pl.ds(s + 1, 1), :] = sums[0:1, BLOCK:]
            return carry

        lax.fori_loop(0, count // 2, pair, 0, unroll=count // 2)

    run(0, EARLY, early_cost_ref, early_coef_ref)
    load_cost.wait()
    load_coef.wait()
    run(EARLY, LATE, late_cost_ref, late_coef_ref)
    for s in range(CAP):
        member_out_ref[pl.ds(number_ref[MEMBER + s], 1), :] += sums_ref[s:s + 1, :]


def finish_kernel(recv_ref, m0_ref, m1_ref, m2_ref, m3_ref, capacity_ref, gradient_ref, share_ref):
    share_ref[...] = ((m0_ref[...] + m1_ref[...]) + (m2_ref[...] + m3_ref[...])) * (1.0 / BLOCK)
    low = lax.broadcasted_iota(jnp.int32, (8, BLOCK), 1) < BLOCK // 2
    totals = [jnp.zeros((8, BLOCK), jnp.float32) for _ in range(JB_DEV)]
    for i in range(0, MEM, 8):
        first, second, named = (recv_ref[i:i + 8, 0, j * BLOCK:(j + 1) * BLOCK] for j in range(ROWS))
        turned = pltpu.roll(named, BLOCK // 2, 1)
        name_first = jnp.where(low, named, turned)
        name_second = jnp.where(low, turned, named)
        for k in range(JB_DEV):
            totals[k] = totals[k] + jnp.where(name_first == float(k), first, 0.0)
            totals[k] = totals[k] + jnp.where(name_second == float(k), second, 0.0)
    summed = jnp.concatenate([jnp.sum(t, axis=0, keepdims=True) for t in totals], axis=0)
    gradient_ref[...] = summed - capacity_ref[...].astype(jnp.float32)


def stage(owner, local, member, cost, coef):
    early = pltpu.VMEM((EARLY, BLOCK, BLOCK), jnp.bfloat16)
    return pl.pallas_call(
        stage_kernel,
        out_shape=(
            early,
            early,
            pltpu.VMEM((MEM * ROWS, 1, BLOCK), jnp.float32),
            jax.ShapeDtypeStruct((4 * CAP,), jnp.int32),
        ),
        in_specs=[SMEM] * 3 + [ANY] * 2,
        out_specs=(VMEM, VMEM, VMEM, SMEM),
        scratch_shapes=[pltpu.SMEM((MEM,), jnp.int32), pltpu.SemaphoreType.DMA((2,))],
        compiler_params=pltpu.CompilerParams(vmem_limit_bytes=4 * 1024 * 1024),
        cost_estimate=pl.CostEstimate(flops=0, bytes_accessed=8 * EARLY * BLOCK * BLOCK, transcendentals=0),
        name="stage",
    )(owner, local, member, in_hbm(cost), in_hbm(coef))


def stage_late(cost, coef):
    late = pltpu.VMEM((LATE, BLOCK, BLOCK), jnp.bfloat16)
    return pl.pallas_call(
        stage_late_kernel,
        out_shape=(late, late),
        in_specs=[ANY] * 2,
        out_specs=(VMEM, VMEM),
        scratch_shapes=[pltpu.SemaphoreType.DMA((2,))],
        compiler_params=pltpu.CompilerParams(vmem_limit_bytes=4 * 1024 * 1024),
        cost_estimate=pl.CostEstimate(flops=0, bytes_accessed=8 * LATE * BLOCK * BLOCK, transcendentals=0),
        name="stage_late",
    )(in_hbm(cost), in_hbm(coef))


def columns(number, *blocks):
    return pl.pallas_call(
        columns_kernel,
        out_shape=(
            jax.ShapeDtypeStruct((MEM * ROWS, 1, BLOCK), jnp.float32),
            pltpu.VMEM((CAP, BLOCK), jnp.float32),
        ),
        in_specs=[SMEM] + [VMEM] * 7,
        out_specs=(VMEM, VMEM),
        scratch_shapes=[pltpu.VMEM((CAP * 8, BLOCK), jnp.float32), pltpu.VMEM((CAP, BLOCK), jnp.float32)],
        compiler_params=pltpu.CompilerParams(vmem_limit_bytes=8 * MIB),
        cost_estimate=pl.CostEstimate(
            flops=6 * CAP * BLOCK * BLOCK, bytes_accessed=4 * CAP * BLOCK * BLOCK, transcendentals=0
        ),
        name="columns",
    )(number, *map(in_vmem, blocks))


def primal_and_members(number, minus, early_cost, early_coef, cost, coef):
    late = pltpu.VMEM((LATE, BLOCK, BLOCK), jnp.bfloat16)
    return pl.pallas_call(
        primal_kernel,
        out_shape=(pltpu.VMEM((CAP, BLOCK, BLOCK), jnp.bfloat16), pltpu.VMEM((MB_DEV, BLOCK), jnp.float32)),
        in_specs=[SMEM] + [VMEM] * 3 + [ANY] * 2,
        out_specs=(VMEM, VMEM),
        scratch_shapes=[late, late, pltpu.VMEM((CAP, BLOCK), jnp.float32), pltpu.SemaphoreType.DMA((2,))],
        compiler_params=pltpu.CompilerParams(vmem_limit_bytes=8 * MIB),
        cost_estimate=pl.CostEstimate(
            flops=6 * CAP * BLOCK * BLOCK, bytes_accessed=6 * CAP * BLOCK * BLOCK, transcendentals=0
        ),
        name="primal",
    )(number, in_vmem(minus), in_vmem(early_cost), in_vmem(early_coef), in_hbm(cost), in_hbm(coef))


def finish(recv, share, others, capacity):
    return pl.pallas_call(
        finish_kernel,
        out_shape=(
            jax.ShapeDtypeStruct((JB_DEV, BLOCK), jnp.float32),
            jax.ShapeDtypeStruct((MB_DEV, BLOCK), jnp.float32),
        ),
        in_specs=[VMEM] * 6,
        out_specs=(VMEM, VMEM),
        compiler_params=pltpu.CompilerParams(vmem_limit_bytes=2 * 1024 * 1024),
        name="finish",
    )(recv, share, *others, capacity)


def per_device(pair_cost, pair_coef, slot_member, slot_owner, slot_local, duals, capacity):
    copies = spread(duals)
    rows = lax.all_to_all(copies, ("z", "y"), split_axis=0, concat_axis=0, tiled=True).reshape(HALF, BLOCK)
    cost, coef, named, number = stage(
        slot_owner.reshape(1, CAP), slot_local, slot_member, pair_cost, pair_coef
    )
    rows, number, late_cost, late_coef = lax.optimization_barrier((rows, number, pair_cost, pair_coef))
    other_rows = lax.ppermute(rows, "c", [(0, 1), (1, 0)])
    late_cost, late_coef = stage_late(late_cost, late_coef)
    send, minus = columns(number, named, rows, other_rows, cost, coef, late_cost, late_coef)
    send = send.reshape(MEM, 1, ROWS * BLOCK)
    recv = lax.all_to_all(send, ("z", "y", "c"), split_axis=0, concat_axis=0, tiled=True)
    primal, share = primal_and_members(number, minus, cost, coef, pair_cost, pair_coef)
    others = [lax.ppermute(share, "x", [(i, i ^ k) for i in range(X)]) for k in (1, 2, 3)]
    gradient, share = finish(recv, share, others, capacity)
    return primal, gradient, share


def solution(mesh):
    axes = ("z", "y", "c", "x")
    fine = Mesh(mesh.devices.reshape(Z, Y, C, X), axes)
    each = lambda n: P(axes, *([None] * (n - 1)))
    return jax.shard_map(
        per_device,
        mesh=fine,
        in_specs=(each(3), each(3), each(2), each(3), each(2), each(2), each(2)),
        out_specs=(each(3), each(2), P(("z", "y", "c"), None)),
        check_vma=False,
    )
```
